32 devices in a mesh: cell: 4 (over x, core), gene: 8 (over z, y).
Axes of the slice: x: 2, y: 2, z: 4, core: 2. Of those that a mesh axis runs over, the one named last changes fastest.
Arguments:
- query_rows: bfloat16 [4, 1024, 1536], P('cell', 'gene'), may hold values from -1.5 to 1.5
- key_rows: bfloat16 [4, 1024, 1536], P('cell', 'gene'), may hold values from -1.5 to 1.5
- value_rows: bfloat16 [4, 1024, 1536], P('cell', 'gene'), may hold values from -6 to 6
- output_rows: bfloat16 [4, 1024, 1536], P('cell', 'gene'), may hold values from -6 to 6
- output_grad: bfloat16 [4, 1024, 1536], P('cell', 'gene'), may hold values from -6 to 6
- row_lse: float32 [4, 1024, 12], P('cell', 'gene'), may hold values from 3 to 6
- block_bias: float32 [8, 12, 8], replicated, may hold values from -1.5 to 1.5
- block_index: int32 [8, 8], replicated, may hold values from 0 to 7, each once within a row
- block_count: int32 [8], replicated, may hold values from 1 to 8, 32 in all
Outputs:
- query_grad: bfloat16 [4, 1024, 1536], P('cell', 'gene')
- key_grad: bfloat16 [4, 1024, 1536], P('cell', 'gene')
- value_grad: bfloat16 [4, 1024, 1536], P('cell', 'gene')
- bias_grad: float32 [8, 12, 8], P('gene', None, 'cell')
The draws below stay inside these ranges and needn't reach their ends.
Inputs may be any that keep to these rules, and one draw needn't show every extreme that they name: Each row of block_index lists every key block once; its first block_count entries are the listed ones, and one row block lists all 8. `block_count`: one row block has 8 listed key blocks.
All inputs are finite; a program needn't handle non-finite values.
Results may differ from the reference program's by a relative error of at most 0.0049.
Values may be sent and summed in bfloat16 or wider, within the bound.
No kernel may reach another device: no remote copies, remote signals or barrier semaphores. Data moves between devices by JAX's collectives and lax.ppermute only.
A program may use at most 128 MiB of HBM per device.

```python
import math
import jax
import jax.numpy as jnp
import numpy as np
from jax import lax

BLOCK = 128
HEADS = 12
HEAD_DIM = 128
NB = 8
GENES = 1024
CELLS = 4


def block_levels(own_key, extent, pieces, least, largest):
    factor_of = 1.0
    for axis_at, parts in pieces:
        draws = jax.random.uniform(jax.random.fold_in(jax.random.fold_in(own_key, 6), axis_at), (parts,), jnp.float32, least / len(pieces), largest / len(pieces))
        factor_of = factor_of * jnp.repeat(jnp.exp(draws), extent[axis_at] // parts).reshape((-1,) + (1,) * (len(extent) - 1 - axis_at))
    return factor_of


def profile(count, total, bound, slope):
    portions = [(1 << 20) // math.isqrt(standing ** slope) + 1 for standing in range(2, count + 1)]
    spare, given = total - bound - (count - 1), [1] * (count - 1)
    while spare > 0:
        movable = [i for i in range(count - 1) if given[i] < bound]
        whole, budget = sum([portions[i] for i in movable]), spare
        for i in movable:
            extra = min(bound - given[i], max(1, budget * portions[i] // whole), spare)
            given[i] = given[i] + extra
            spare = spare - extra
    return np.array([bound] + given)


def uneven(rng, number_of, total, bound, lean):
    if number_of == 2:
        one = jax.random.randint(rng, (), max(1, total - bound), min(bound, total - 1) + 1)
        return jnp.stack([one, total - one])
    tallies = jnp.asarray(profile(number_of, total, bound, lean), jnp.int32)
    pairs = (number_of - 1) // 2
    source_of, receiver = tallies[1:1 + 2 * pairs:2], tallies[2:2 + 2 * pairs:2]
    slack = jnp.minimum(source_of - 1, bound - receiver)
    passed = jax.random.randint(jax.random.fold_in(rng, 1), (pairs,), 0, 1 << 20) % (slack + 1)
    tallies = tallies.at[1:1 + 2 * pairs:2].set(source_of - passed).at[2:2 + 2 * pairs:2].set(receiver + passed)
    return tallies[jax.random.permutation(jax.random.fold_in(rng, 2), number_of)]


def centred(stream_key, shape, spread, bound, split=(), kind=jnp.bfloat16):
    loudness = block_levels(stream_key, shape, split, -0.22, 0.18) if split else 1.0
    entries = jax.random.normal(stream_key, shape, jnp.float32) * spread * loudness
    return jnp.minimum(jnp.maximum(entries, -bound), bound).astype(kind)


def setup_inputs(seed: int = 0) -> dict:
    key_of = jax.random.split(jax.random.key(seed), 10)
    query_rows = jnp.clip(jax.random.uniform(key_of[0], (CELLS, GENES, HEADS * HEAD_DIM), jnp.float32, -1.5, 1.5) * block_levels(key_of[0], (CELLS, GENES, HEADS * HEAD_DIM), ((0, 4), (1, 8)), -0.4, 0.0), -1.5, 1.5).astype(jnp.bfloat16)
    key_rows = jnp.clip(jax.random.uniform(key_of[1], (CELLS, GENES, HEADS * HEAD_DIM), jnp.float32, -1.5, 1.5) * block_levels(key_of[1], (CELLS, GENES, HEADS * HEAD_DIM), ((0, 4), (1, 8)), -0.4, 0.0), -1.5, 1.5).astype(jnp.bfloat16)
    value_rows = centred(key_of[2], (CELLS, GENES, HEADS * HEAD_DIM), 1.0, 6.0, ((0, 4), (1, 8)))
    output_rows = centred(key_of[3], (CELLS, GENES, HEADS * HEAD_DIM), 1.0, 6.0, ((0, 4), (1, 8)))
    output_grad = centred(key_of[4], (CELLS, GENES, HEADS * HEAD_DIM), 1.0, 6.0, ((0, 4), (1, 8)))
    row_lse = jnp.clip(3.0 + 3.0 * jax.random.uniform(key_of[5], (CELLS, GENES, HEADS), jnp.float32) ** block_levels(key_of[5], (CELLS, GENES, HEADS), ((0, 4), (1, 8)), -0.2, 0.2), 3.0, 6.0)
    block_bias = jnp.clip(jax.random.uniform(key_of[6], (NB, HEADS, NB), jnp.float32, -1.5, 1.5), -1.5, 1.5)
    block_index = jax.vmap(lambda own: jax.random.permutation(own, NB))(jax.random.split(key_of[7], NB)).reshape((NB, NB)).astype(jnp.int32)
    block_count = uneven(key_of[8], NB, NB * NB // 2, NB, 2).astype(jnp.int32)
    return dict(query_rows=query_rows, key_rows=key_rows, value_rows=value_rows, output_rows=output_rows, output_grad=output_grad, row_lse=row_lse, block_bias=block_bias, block_index=block_index, block_count=block_count)


def pair_tables(block_bias, block_index, block_count):
    block_total = block_bias.shape[0]
    columns = jnp.arange(block_total, dtype=jnp.int32)
    slot_live = jnp.arange(block_index.shape[1], dtype=jnp.int32)[None, :] < block_count[:, None]
    listed = ((block_index[:, :, None] == columns[None, None, :]) & slot_live[:, :, None]).astype(jnp.float32)
    pair_bias = jnp.einsum('ihs,isj->hij', block_bias, listed, precision=lax.Precision.HIGHEST)
    pair_mask = lax.optimization_barrier(jnp.sum(listed, axis=1))
    return (listed, pair_bias, pair_mask)

def reference(query_rows, key_rows, value_rows, output_rows, output_grad, row_lse, block_bias, block_index, block_count):
    score_scale = 1.0 / math.sqrt(HEAD_DIM)
    listed, pair_bias, pair_mask = pair_tables(block_bias, block_index, block_count)
    full_bias = jnp.repeat(jnp.repeat(pair_bias, BLOCK, axis=1), BLOCK, axis=2)
    full_mask = jnp.repeat(jnp.repeat(pair_mask, BLOCK, axis=0), BLOCK, axis=1) > 0.5

    def one_cell(inputs):
        query, keyset, valueset, output, grad, lse = inputs
        shape = (GENES, HEADS, HEAD_DIM)
        query = query.astype(jnp.float32).reshape(shape)
        keyset = keyset.astype(jnp.float32).reshape(shape)
        valueset = valueset.astype(jnp.float32).reshape(shape)
        output = output.astype(jnp.float32).reshape(shape)
        grad = grad.astype(jnp.float32).reshape(shape)
        scores = jnp.einsum('rhd,khd->hrk', query, keyset) * score_scale + full_bias
        weights = jnp.where(full_mask[None], jnp.exp(scores - jnp.transpose(lse)[:, :, None]), 0.0)
        row_delta = jnp.transpose(lax.optimization_barrier(jnp.sum(grad * output, axis=-1)))
        weight_grads = jnp.einsum('rhd,khd->hrk', grad, valueset)
        score_grads = weights * (weight_grads - row_delta[:, :, None])
        weights_low = lax.optimization_barrier(weights.astype(jnp.bfloat16)).astype(jnp.float32)
        grads_low = lax.optimization_barrier(score_grads.astype(jnp.bfloat16)).astype(jnp.float32)
        value_grad = jnp.einsum('hrk,rhd->khd', weights_low, grad)
        query_grad = jnp.einsum('hrk,khd->rhd', grads_low, keyset) * score_scale
        key_grad = jnp.einsum('hrk,rhd->khd', grads_low, query) * score_scale
        block_sums = score_grads.reshape(HEADS, NB, BLOCK, NB, BLOCK).sum(axis=(2, 4))
        flat = (GENES, HEADS * HEAD_DIM)
        return (query_grad.reshape(flat).astype(jnp.bfloat16), key_grad.reshape(flat).astype(jnp.bfloat16), value_grad.reshape(flat).astype(jnp.bfloat16), block_sums)
    query_grad, key_grad, value_grad, block_sums = lax.map(one_cell, (query_rows, key_rows, value_rows, output_rows, output_grad, row_lse))
    bias_grad = jnp.einsum('hij,isj->ihs', lax.optimization_barrier(jnp.sum(block_sums, axis=0)), listed, precision=lax.Precision.HIGHEST)
    return (query_grad, key_grad, value_grad, bias_grad)
```

```python
import functools
import math

import jax
import jax.numpy as jnp
from jax import lax
from jax.experimental import pallas as pl
from jax.experimental.pallas import tpu as pltpu
from jax.sharding import PartitionSpec as P

BLOCK = 128
STAT_ROWS = 16
SUM_ROWS = 16
VMEM_LIMIT = 56 * 1024 * 1024


def split_three(row):
    high = row.astype(jnp.bfloat16).astype(jnp.float32)
    middle = (row - high).astype(jnp.bfloat16).astype(jnp.float32)
    return [high, middle, row - high - middle]


def pack_far_kernel(plan, query, output, grad, lse, *outs):
    members, width, head_size = plan["members"], plan["width"], plan["head_size"]
    mine = lax.axis_index("gene") % members
    for hop in range(members):
        owner = mine ^ hop
        columns = pl.ds(pl.multiple_of(owner * width, head_size), width)
        grad_part, target = grad[0, :, columns], outs[hop]
        products = grad_part.astype(jnp.float32) * output[0, :, columns].astype(jnp.float32)
        target[0:BLOCK, :] = query[0, :, columns]
        target[BLOCK : 2 * BLOCK, :] = grad_part
        for head in range(plan["share"]):
            lanes = slice(head * head_size, (head + 1) * head_size)
            delta = jnp.sum(jnp.transpose(products[:, lanes]), axis=0, keepdims=True)
            saved = lse[0, pl.ds(owner * plan["share"] + head, 1), :]
            rows = split_three(saved) + split_three(delta)
            rows.append(jnp.zeros((STAT_ROWS - 6, BLOCK), jnp.float32))
            stats = jnp.concatenate(rows, axis=0).astype(jnp.bfloat16)
            target[2 * BLOCK : 2 * BLOCK + STAT_ROWS, lanes] = stats


def pack_near_kernel(plan, key, value, *refs):
    members, width, head_size = plan["members"], plan["width"], plan["head_size"]
    mine = lax.axis_index("gene") % members
    base = 2 * BLOCK + STAT_ROWS
    for hop in range(members):
        columns = pl.ds(pl.multiple_of((mine ^ hop) * width, head_size), width)
        near = refs[members + hop]
        near[0:base, :] = refs[hop][...]
        near[base : base + BLOCK, :] = key[0, :, columns]
        near[base + BLOCK : base + 2 * BLOCK, :] = value[0, :, columns]


def table_kernel(plan, bias, index, count, bias_out, mask_out):
    members, share, blocks = plan["members"], plan["share"], plan["blocks"]
    heads = members * share
    me = lax.axis_index("gene")
    mine = me % members
    for hop in range(blocks):
        row = me ^ hop
        for side in range(members):
            mask_out[hop * members + side] = 0
            for head in range(share):
                bias_out[(head * blocks + hop) * members + side] = 0.0

        def listed(slot, carry, hop=hop, row=row):
            column = index[row * blocks + slot]
            side = column ^ me

            @pl.when(side < members)
            def _():
                mask_out[hop * members + side] = 1
                for head in range(share):
                    bias_out[(head * blocks + hop) * members + side] = bias[
                        (row * heads + mine * share + head) * blocks + slot
                    ]

            return carry

        lax.fori_loop(0, count[row], listed, 0)


def stage_kernel(plan, first, last, bias, mask, *refs):
    blocks, members, share = plan["blocks"], plan["members"], plan["share"]
    head_size, scale = plan["head_size"], plan["scale"]
    count = last - first
    near = refs[:members]
    rest = refs[members:]
    if first == 0:
        pieces = near
        outs, sum_refs, rest = rest[:count], rest[count : count + 2], rest[count + 2 :]
        grads_out = None
    else:
        pieces, sum_refs, rest = rest[:count], rest[count : count + 2], rest[count + 2 :]
        outs, grads_out, rest = rest[:count], rest[count : count + members], rest[count + members :]
    weights_low, grads_low = rest
    base = 2 * BLOCK + STAT_ROWS
    nt = (((1,), (1,)), ((), ()))
    nn = (((1,), (0,)), ((), ()))
    tn = (((0,), (0,)), ((), ()))
    dot = functools.partial(lax.dot_general, preferred_element_type=jnp.float32)

    def one_head(head, carry):
        lanes = pl.ds(pl.multiple_of(head * head_size, head_size), head_size)
        keys = jnp.concatenate([near[s][base : base + BLOCK, lanes] for s in range(members)], axis=0)
        values = jnp.concatenate(
            [near[s][base + BLOCK : base + 2 * BLOCK, lanes] for s in range(members)], axis=0
        )
        for hop in range(count):
            piece = pieces[hop]
            scores = dot(keys, piece[0:BLOCK, lanes], nt)
            weight_grads = dot(values, piece[BLOCK : 2 * BLOCK, lanes], nt)
            stats = piece[2 * BLOCK : base, lanes].astype(jnp.float32)
            saved = stats[0:1] + stats[1:2] + stats[2:3]
            delta = stats[3:4] + stats[4:5] + stats[5:6]
            place = slice(hop * BLOCK, (hop + 1) * BLOCK)
            rows = []
            for side in range(members):
                part = slice(side * BLOCK, (side + 1) * BLOCK)
                at = (first + hop) * members + side
                live = mask[at] > 0
                shift = bias[head * (blocks * members) + at] - saved
                grown = jnp.exp(scores[part] * scale + shift)
                weights = jnp.where(live, grown, 0.0)
                score_grads = weights * (weight_grads[part] - delta)
                weights_low[part, place] = weights.astype(jnp.bfloat16)
                grads_low[part, place] = score_grads.astype(jnp.bfloat16)
                rows += split_three(jnp.sum(score_grads, axis=0, keepdims=True))
            rows.append(jnp.zeros((SUM_ROWS - 3 * members, BLOCK), jnp.float32))
            outs[hop][BLOCK : BLOCK + SUM_ROWS, lanes] = jnp.concatenate(rows, axis=0).astype(
                jnp.bfloat16
            )
        queries = jnp.concatenate([piece[0:BLOCK, lanes] for piece in pieces], axis=0)
        grads = jnp.concatenate([piece[BLOCK : 2 * BLOCK, lanes] for piece in pieces], axis=0)
        value_grad = dot(weights_low[...], grads, nn)
        key_grad = dot(grads_low[...], queries, nn)
        query_grad = dot(grads_low[...], keys, tn) * scale
        for hop in range(count):
            part = slice(hop * BLOCK, (hop + 1) * BLOCK)
            outs[hop][0:BLOCK, lanes] = query_grad[part].astype(jnp.bfloat16)
        if grads_out is None:
            sum_refs[0][:, lanes] = key_grad
            sum_refs[1][:, lanes] = value_grad
        else:
            key_grad = (key_grad + sum_refs[0][:, lanes]) * scale
            value_grad = value_grad + sum_refs[1][:, lanes]
            for hop in range(members):
                part = slice(hop * BLOCK, (hop + 1) * BLOCK)
                grads_out[hop][0:BLOCK, lanes] = key_grad[part].astype(jnp.bfloat16)
                grads_out[hop][BLOCK : 2 * BLOCK, lanes] = value_grad[part].astype(jnp.bfloat16)
        return carry

    lax.fori_loop(0, share, one_head, 0)


def query_kernel(plan, index, *refs):
    blocks, members, share = plan["blocks"], plan["members"], plan["share"]
    width, head_size = plan["width"], plan["head_size"]
    pieces = refs[:blocks]
    query_grad, bias_out, slots, sums = refs[blocks:]
    me = lax.axis_index("gene")
    mine = me % members
    for slot in range(blocks):
        slots[index[me * blocks + slot]] = slot
    for hop in range(members):
        owner = mine ^ hop
        columns = pl.ds(pl.multiple_of(owner * width, head_size), width)
        total = jnp.zeros((BLOCK, width), jnp.float32)
        for other in range(hop, blocks, members):
            total = total + pieces[other][0:BLOCK, :].astype(jnp.float32)
            for head in range(share):
                lanes = slice(head * head_size, (head + 1) * head_size)
                rows = pieces[other][BLOCK : BLOCK + SUM_ROWS, lanes].astype(jnp.float32)
                for side in range(members):
                    slot = slots[me ^ other ^ side]
                    sums[pl.ds((owner * share + head) * blocks + slot, 1), :] = (
                        rows[3 * side : 3 * side + 1]
                        + rows[3 * side + 1 : 3 * side + 2]
                        + rows[3 * side + 2 : 3 * side + 3]
                    )
        query_grad[0, :, columns] = total.astype(jnp.bfloat16)
    bias_out[...] = jnp.sum(jnp.transpose(sums[...]), axis=0, keepdims=True)


def owner_kernel(plan, *refs):
    members, width, head_size = plan["members"], plan["width"], plan["head_size"]
    pieces = refs[:members]
    key_grad, value_grad = refs[members:]
    mine = lax.axis_index("gene") % members
    for hop in range(members):
        columns = pl.ds(pl.multiple_of((mine ^ hop) * width, head_size), width)
        key_grad[0, :, columns] = pieces[hop][0:BLOCK, :]
        value_grad[0, :, columns] = pieces[hop][BLOCK : 2 * BLOCK, :]


def call(kernel, outs, scratch=(), smem_in=0, smem_out=False, count=0):
    places = [pl.BlockSpec(memory_space=pltpu.SMEM)] * smem_in
    places += [pl.BlockSpec(memory_space=pltpu.VMEM)] * count
    space = pltpu.SMEM if smem_out else pltpu.VMEM
    return pl.pallas_call(
        kernel,
        out_shape=outs,
        in_specs=places,
        out_specs=[pl.BlockSpec(memory_space=space)] * len(outs),
        scratch_shapes=list(scratch),
        compiler_params=pltpu.CompilerParams(vmem_limit_bytes=VMEM_LIMIT),
    )


def shards(
    query_rows,
    key_rows,
    value_rows,
    output_rows,
    output_grad,
    row_lse,
    block_bias,
    block_index,
    block_count,
):
    row_width = query_rows.shape[2]
    head_count = row_lse.shape[2]
    blocks = block_bias.shape[0]
    members = math.gcd(blocks, head_count)
    share = head_count // members
    head_size = row_width // head_count
    width = share * head_size
    plan = dict(
        blocks=blocks,
        members=members,
        share=share,
        head_size=head_size,
        width=width,
        scale=1.0 / math.sqrt(head_size),
    )
    low, full = jnp.bfloat16, jnp.float32
    base = 2 * BLOCK + STAT_ROWS
    near = jax.ShapeDtypeStruct((base + 2 * BLOCK, width), low)
    far = jax.ShapeDtypeStruct((base, width), low)

    def move(array, hop):
        return lax.ppermute(array, "gene", [(i, i ^ hop) for i in range(blocks)])

    far_sent = call(functools.partial(pack_far_kernel, plan), [far] * members, count=4)(
        query_rows, output_rows, output_grad, jnp.transpose(row_lse, (0, 2, 1))
    )
    near_sent = call(functools.partial(pack_near_kernel, plan), [near] * members, count=2 + members)(
        key_rows, value_rows, *far_sent
    )
    far_pieces = [move(far_sent[hop % members], hop) for hop in range(members, blocks)]
    near_pieces = [near_sent[0]] + [move(near_sent[hop], hop) for hop in range(1, members)]
    tables = call(
        functools.partial(table_kernel, plan),
        [
            jax.ShapeDtypeStruct((share * blocks * members,), full),
            jax.ShapeDtypeStruct((blocks * members,), jnp.int32),
        ],
        smem_in=3,
        smem_out=True,
    )(block_bias.reshape(-1), block_index.reshape(-1), block_count)
    query_out = jax.ShapeDtypeStruct((BLOCK + SUM_ROWS, width), low)
    owner_out = jax.ShapeDtypeStruct((2 * BLOCK, width), low)
    partial = jax.ShapeDtypeStruct((members * BLOCK, width), full)

    def stage(first, last, outs, *arrays):
        scratch = pltpu.VMEM((members * BLOCK, (last - first) * BLOCK), low)
        return call(
            functools.partial(stage_kernel, plan, first, last),
            outs,
            scratch=[scratch, scratch],
            smem_in=2,
            count=len(arrays),
        )(*tables, *arrays)

    made = stage(0, members, [query_out] * members + [partial] * 2, *near_pieces)
    near_query, partials = made[:members], made[members:]
    near_query = [near_query[0]] + [move(near_query[hop], hop) for hop in range(1, members)]
    made = stage(
        members,
        blocks,
        [query_out] * (blocks - members) + [owner_out] * members,
        *near_pieces,
        *far_pieces,
        *partials,
    )
    far_query = [move(made[hop - members], hop) for hop in range(members, blocks)]
    owned = made[blocks - members :]
    owned = [owned[0]] + [move(owned[hop], hop) for hop in range(1, members)]
    whole = jax.ShapeDtypeStruct((1, BLOCK, row_width), low)
    query_grad, sums = call(
        functools.partial(query_kernel, plan),
        [whole, jax.ShapeDtypeStruct((1, head_count * blocks), full)],
        scratch=[pltpu.SMEM((blocks,), jnp.int32), pltpu.VMEM((head_count * blocks, BLOCK), full)],
        smem_in=1,
        count=blocks,
    )(block_index.reshape(-1), *near_query, *far_query)
    key_grad, value_grad = call(functools.partial(owner_kernel, plan), [whole] * 2, count=members)(
        *owned
    )
    bias_grad = lax.psum_scatter(
        sums.reshape(1, head_count, blocks), "cell", scatter_dimension=2, tiled=True
    )
    return (query_grad, key_grad, value_grad, bias_grad)


def solution(mesh):
    rows = P("cell", "gene", None)
    in_specs = (rows,) * 6 + (P(),) * 3
    out_specs = (rows, rows, rows, P("gene", None, "cell"))
    return jax.shard_map(shards, mesh=mesh, in_specs=in_specs, out_specs=out_specs, check_vma=False)
```

```python
import functools
import math

import jax
import jax.numpy as jnp
from jax import lax
from jax.experimental import pallas as pl
from jax.experimental.pallas import tpu as pltpu
from jax.sharding import PartitionSpec as P

BLOCK = 128
ROW_TILE = 16
VMEM_LIMIT = 60 * 1024 * 1024
STAGE_LIMIT = 40 * 1024 * 1024
FAR_STAGES = 1
LOG2E = math.log2(math.e)
UNLISTED = -1e30


def split_two(row):
    high = row.astype(jnp.bfloat16).astype(jnp.float32)
    return [high, row - high]


def pack_kernel(plan, query, key, value, output, grad, lse, *outs):
    members, share, head_size = plan["members"], plan["share"], plan["head_size"]
    width, stat_rows = share * head_size, plan["stat_rows"]
    mine = lax.axis_index("gene") % members
    for hop in range(members):
        owner = mine ^ hop
        near, far = outs[members].at[owner], outs[hop]
        start = pl.multiple_of(owner * width, head_size)
        rows = []
        for head in range(share):
            columns = pl.ds(start + head * head_size, head_size)
            query_part, grad_part = query[0, :, columns], grad[0, :, columns]
            products = grad_part.astype(jnp.float32) * output[0, :, columns].astype(jnp.float32)
            top = 2 * BLOCK * head
            far[top : top + BLOCK, :] = query_part
            far[top + BLOCK : top + 2 * BLOCK, :] = grad_part
            top = 4 * BLOCK * head
            near[top : top + BLOCK, :] = query_part
            near[top + BLOCK : top + 2 * BLOCK, :] = grad_part
            near[top + 2 * BLOCK : top + 3 * BLOCK, :] = key[0, :, columns]
            near[top + 3 * BLOCK : top + 4 * BLOCK, :] = value[0, :, columns]
            delta = jnp.sum(jnp.transpose(products), axis=0, keepdims=True)
            rows += split_two(lse[owner * share + head]) + split_two(delta)
        rows.append(jnp.zeros((stat_rows - 4 * share, BLOCK), jnp.float32))
        stats = jnp.concatenate(rows, axis=0).astype(jnp.bfloat16)
        far[2 * BLOCK * share : 2 * BLOCK * share + stat_rows, :] = stats
        near[4 * BLOCK * share : 4 * BLOCK * share + stat_rows, :] = stats


def table_kernel(plan, bias, index, count, shift):
    members, share, blocks = plan["members"], plan["share"], plan["blocks"]
    heads = members * share
    me = lax.axis_index("gene")
    mine = me % members
    for place in range(blocks):
        row = me ^ place
        for at in range(members * share):
            shift[place * members * share + at] = UNLISTED

        def listed(slot, carry, place=place, row=row):
            side = index[row * blocks + slot] ^ me

            @pl.when(side < members)
            def _():
                for head in range(share):
                    shift[(place * members + side) * share + head] = LOG2E * bias[
                        (row * heads + mine * share + head) * blocks + slot
                    ]

            return carry

        lax.fori_loop(0, count[row], listed, 0)


def stage_kernel(plan, places, first, last, shift, *refs):
    members, share, scale = plan["members"], plan["share"], plan["scale"]
    count = len(places)
    mine = lax.axis_index("gene") % members
    near, rest = [refs[0].at[mine ^ hop] for hop in range(members)], refs[1:]
    fresh = [place for place in places if place >= members]
    pieces = [near[place] for place in places if place < members] + list(rest[: len(fresh)])
    steps = [(4 if place < members else 2) * BLOCK for place in places]
    rest = rest[len(fresh) :]
    before = None
    if not first:
        before, rest = rest[:2], rest[2:]
    outs, rest = rest[:count], rest[count:]
    if last:
        owned, rest = rest[:members], rest[members:]
    else:
        after, rest = rest[:2], rest[2:]
    weights_low, grads_low, sums = rest
    nt = (((1,), (1,)), ((), ()))
    nn = (((1,), (0,)), ((), ()))
    tn = (((0,), (0,)), ((), ()))
    dot = functools.partial(lax.dot_general, preferred_element_type=jnp.float32)
    stats = [
        piece[step * share : step * share + plan["stat_rows"], :].astype(jnp.float32)
        for piece, step in zip(pieces, steps)
    ]
    wide = 2 if count % 2 == 0 else 1
    total_rows = share * members
    if plan["sum_rows"] > total_rows:
        for at in range(count):
            sums[at, total_rows:, :] = jnp.zeros((plan["sum_rows"] - total_rows, BLOCK), jnp.float32)

    def own(side, head, which):
        top = 4 * BLOCK * head + (2 + which) * BLOCK
        return near[side][top : top + BLOCK, :]

    def rows(at, head, which):
        top = steps[at] * head + which * BLOCK
        return pieces[at][top : top + BLOCK, :]

    for head in range(share):
        for group in range(0, count, wide):
            ats = range(group, group + wide)
            queries = jnp.concatenate([rows(at, head, 0) for at in ats], axis=0)
            grads = jnp.concatenate([rows(at, head, 1) for at in ats], axis=0)
            line = jnp.concatenate([stats[at][4 * head : 4 * head + 4] for at in ats], axis=1)
            saved = (line[0:1] + line[1:2]) * LOG2E
            delta = line[2:3] + line[3:4]
            spot = slice(group * BLOCK, (group + wide) * BLOCK)
            for side in range(members):
                part = slice(side * BLOCK, (side + 1) * BLOCK)
                scores = dot(own(side, head, 0), queries, nt)
                weight_grads = dot(own(side, head, 1), grads, nt)
                shifts = [
                    jnp.full((1, BLOCK), shift[(places[at] * members + side) * share + head])
                    for at in ats
                ]
                offset = jnp.concatenate(shifts, axis=1) - saved
                weights = jnp.exp2(scores * (scale * LOG2E) + offset)
                score_grads = weights * (weight_grads - delta)
                weights_low[part, spot] = weights.astype(jnp.bfloat16)
                grads_low[part, spot] = score_grads.astype(jnp.bfloat16)
                column_sums = jnp.sum(score_grads, axis=0, keepdims=True)
                row = head * members + side
                for at in ats:
                    lanes = slice((at - group) * BLOCK, (at - group + 1) * BLOCK)
                    sums[at, row : row + 1, :] = column_sums[:, lanes]
        keys = jnp.concatenate([own(side, head, 0) for side in range(members)], axis=0)
        queries = jnp.concatenate([rows(at, head, 0) for at in range(count)], axis=0)
        grads = jnp.concatenate([rows(at, head, 1) for at in range(count)], axis=0)
        query_grad = dot(grads_low[...], keys, tn) * scale
        for at in range(count):
            outs[at][head * BLOCK : (head + 1) * BLOCK, :] = query_grad[
                at * BLOCK : (at + 1) * BLOCK
            ].astype(jnp.bfloat16)
        value_grad = dot(weights_low[...], grads, nn)
        key_grad = dot(grads_low[...], queries, nn)
        if before is not None:
            key_grad = key_grad + before[0][head]
            value_grad = value_grad + before[1][head]
        if last:
            key_grad = key_grad * scale
            top = 2 * BLOCK * head
            for side in range(members):
                part = slice(side * BLOCK, (side + 1) * BLOCK)
                owned[side][top : top + BLOCK, :] = key_grad[part].astype(jnp.bfloat16)
                owned[side][top + BLOCK : top + 2 * BLOCK, :] = value_grad[part].astype(jnp.bfloat16)
        else:
            after[0][head] = key_grad
            after[1][head] = value_grad
    lane = lax.broadcasted_iota(jnp.int32, (plan["sum_rows"], BLOCK), 1)
    for at in range(count):
        total = jnp.sum(sums[at], axis=1, keepdims=True)
        high, low = split_two(total)
        middle, low = split_two(low)
        spread = jnp.where(lane == 1, middle, jnp.where(lane == 2, low, 0.0))
        spread = jnp.where(lane == 0, high, spread)
        outs[at][share * BLOCK : share * BLOCK + plan["sum_rows"], :] = spread.astype(jnp.bfloat16)


def query_kernel(plan, index, *refs):
    blocks, members, share = plan["blocks"], plan["members"], plan["share"]
    head_size, cells = plan["head_size"], plan["cells"]
    heads, per_cell = members * share, blocks // cells
    pieces, query_grad, parts = refs[:blocks], refs[blocks], refs[blocks + 1 : blocks + 1 + cells]
    slots, sums, table = refs[blocks + 1 + cells :]
    me, cell = lax.axis_index("gene"), lax.axis_index("cell")
    mine = me % members
    for slot in range(blocks):
        slots[index[me * blocks + slot]] = slot
    for hop in range(members):
        owner = mine ^ hop
        for other in range(hop, blocks, members):
            rows = pieces[other][share * BLOCK : share * BLOCK + plan["sum_rows"], :]
            rows = rows.astype(jnp.float32)
            for side in range(members):
                slot = slots[me ^ other ^ side]
                for head in range(share):
                    at = head * members + side
                    sums[pl.ds(slot * heads + owner * share + head, 1), :] = rows[at : at + 1]
    line = jnp.sum(jnp.transpose(sums[...]), axis=0, keepdims=True)
    for slot in range(blocks):
        table[slot : slot + 1, 0:heads] = line[:, slot * heads : (slot + 1) * heads]
    for hop in range(cells):
        for slot in range(per_cell):
            parts[hop][slot : slot + 1, :] = table[pl.ds((cell ^ hop) * per_cell + slot, 1), 0:heads]
    for hop in range(members):
        start = pl.multiple_of((mine ^ hop) * (share * head_size), head_size)
        for head in range(share):
            top = head * BLOCK
            total = pieces[hop][top : top + BLOCK, :].astype(jnp.float32)
            for other in range(members + hop, blocks, members):
                total = total + pieces[other][top : top + BLOCK, :].astype(jnp.float32)
            columns = pl.ds(start + head * head_size, head_size)
            query_grad[0, :, columns] = total.astype(jnp.bfloat16)


def owner_kernel(plan, *refs):
    members, share, head_size = plan["members"], plan["share"], plan["head_size"]
    key_grad, value_grad = refs[members:]
    mine = lax.axis_index("gene") % members
    for hop in range(members):
        start = pl.multiple_of((mine ^ hop) * (share * head_size), head_size)
        for head in range(share):
            columns, top = pl.ds(start + head * head_size, head_size), 2 * BLOCK * head
            key_grad[0, :, columns] = refs[hop][top : top + BLOCK, :]
            value_grad[0, :, columns] = refs[hop][top + BLOCK : top + 2 * BLOCK, :]


def call(kernel, outs, scratch=(), smem_in=0, smem_out=False, count=0, limit=VMEM_LIMIT):
    places = [pl.BlockSpec(memory_space=pltpu.SMEM)] * smem_in
    places += [pl.BlockSpec(memory_space=pltpu.VMEM)] * count
    space = pltpu.SMEM if smem_out else pltpu.VMEM
    return pl.pallas_call(
        kernel,
        out_shape=outs,
        in_specs=places,
        out_specs=[pl.BlockSpec(memory_space=space)] * len(outs),
        scratch_shapes=list(scratch),
        compiler_params=pltpu.CompilerParams(vmem_limit_bytes=limit),
    )


def shards(
    query_rows,
    key_rows,
    value_rows,
    output_rows,
    output_grad,
    row_lse,
    block_bias,
    block_index,
    block_count,
):
    row_width = query_rows.shape[2]
    head_count = row_lse.shape[2]
    blocks = block_bias.shape[0]
    members = math.gcd(blocks, head_count)
    share = head_count // members
    head_size = row_width // head_count
    low, full = jnp.bfloat16, jnp.float32
    stat_rows = -(-4 * share // ROW_TILE) * ROW_TILE
    sum_rows = -(-share * members // ROW_TILE) * ROW_TILE
    far_rows = 2 * BLOCK * share + stat_rows
    plan = dict(
        blocks=blocks,
        members=members,
        share=share,
        head_size=head_size,
        stat_rows=stat_rows,
        sum_rows=sum_rows,
        far_rows=far_rows,
        scale=1.0 / math.sqrt(head_size),
    )

    cells = lax.axis_size("cell")
    plan["cells"] = cells
    near_rows = 4 * BLOCK * share + stat_rows
    near_in = jax.ShapeDtypeStruct((members, near_rows, BLOCK), low)
    far_in = jax.ShapeDtypeStruct((far_rows, BLOCK), low)
    sent = call(functools.partial(pack_kernel, plan), [far_in] * members + [near_in], count=6)(
        query_rows, key_rows, value_rows, output_rows, output_grad, jnp.transpose(row_lse, (2, 0, 1))
    )
    groups = [list(range(at, at + members)) for at in range(0, blocks, members)]

    def exchange(array):
        return lax.all_to_all(array, "gene", 0, 0, axis_index_groups=groups)

    def move(array, hop, axis="gene", size=blocks):
        return lax.ppermute(array, axis, [(i, i ^ hop) for i in range(size)])

    far = {hop: move(sent[hop % members], hop) for hop in range(members, blocks)}
    near = exchange(sent[members])
    (table,) = call(
        functools.partial(table_kernel, plan),
        [jax.ShapeDtypeStruct((blocks * members * share,), full)],
        smem_in=3,
        smem_out=True,
    )(block_bias.reshape(-1), block_index.reshape(-1), block_count)
    query_out = jax.ShapeDtypeStruct((share * BLOCK + sum_rows, BLOCK), low)
    partial_out = jax.ShapeDtypeStruct((share, members * BLOCK, BLOCK), full)
    owner_out = jax.ShapeDtypeStruct((2 * BLOCK * share, BLOCK), low)

    def stage(places, first, last, partials):
        count = len(places)
        pieces = [far[place] for place in places if place >= members]
        scratch = pltpu.VMEM((members * BLOCK, count * BLOCK), low)
        made = call(
            functools.partial(stage_kernel, plan, places, first, last),
            [query_out] * count + ([owner_out] * members if last else [partial_out] * 2),
            scratch=[scratch, scratch, pltpu.VMEM((count, sum_rows, BLOCK), full)],
            smem_in=1,
            count=1 + len(pieces) + len(partials),
            limit=STAGE_LIMIT,
        )(table, near, *pieces, *partials)
        return made[:count], made[count:]

    queries, partials, begin = [], [], 0
    for end in (members + (blocks - members) // 2, blocks):
        places = tuple(range(begin, end))
        made, partials = stage(places, begin == 0, end == blocks, partials)
        queries += [move(piece, place) if place else piece for piece, place in zip(made, places)]
        begin = end
    owned = [partials[0]] + [move(partials[hop], hop) for hop in range(1, members)]
    whole = jax.ShapeDtypeStruct((1, BLOCK, row_width), low)
    part_out = jax.ShapeDtypeStruct((blocks // cells, head_count), full)
    query_grad, *parts = call(
        functools.partial(query_kernel, plan),
        [whole] + [part_out] * cells,
        scratch=[
            pltpu.SMEM((blocks,), jnp.int32),
            pltpu.VMEM((head_count * blocks, BLOCK), full),
            pltpu.VMEM((blocks, BLOCK), full),
        ],
        smem_in=1,
        count=blocks,
    )(block_index.reshape(-1), *queries)
    parts = [parts[0]] + [move(parts[hop], hop, "cell", cells) for hop in range(1, cells)]
    key_grad, value_grad = call(functools.partial(owner_kernel, plan), [whole] * 2, count=members)(
        *owned
    )
    bias_grad = jnp.transpose(functools.reduce(jnp.add, parts))[None]
    return (query_grad, key_grad, value_grad, bias_grad)


def solution(mesh):
    rows = P("cell", "gene", None)
    in_specs = (rows,) * 6 + (P(),) * 3
    out_specs = (rows, rows, rows, P("gene", None, "cell"))
    return jax.shard_map(shards, mesh=mesh, in_specs=in_specs, out_specs=out_specs, check_vma=False)
```

```python
import functools
import math

import jax
import jax.numpy as jnp
from jax import lax
from jax.experimental import pallas as pl
from jax.experimental.pallas import tpu as pltpu
from jax.sharding import PartitionSpec as P

BLOCK = 128
ROW_TILE = 16
VMEM_LIMIT = 60 * 1024 * 1024
STAGE_LIMIT = 40 * 1024 * 1024
FAR_STAGES = 1
LOG2E = math.log2(math.e)
UNLISTED = -1e30


def split_two(row):
    high = row.astype(jnp.bfloat16).astype(jnp.float32)
    return [high, row - high]


def pack_kernel(plan, query, key, value, output, grad, lse, *outs):
    members, share, head_size = plan["members"], plan["share"], plan["head_size"]
    width, stat_rows = share * head_size, plan["stat_rows"]
    mine = lax.axis_index("gene") % members
    for hop in range(members):
        owner = mine ^ hop
        near, far = outs[members].at[owner], outs[hop]
        start = pl.multiple_of(owner * width, head_size)
        rows = []
        for head in range(share):
            columns = pl.ds(start + head * head_size, head_size)
            query_part, grad_part = query[0, :, columns], grad[0, :, columns]
            products = grad_part.astype(jnp.float32) * output[0, :, columns].astype(jnp.float32)
            top = 2 * BLOCK * head
            far[top : top + BLOCK, :] = query_part
            far[top + BLOCK : top + 2 * BLOCK, :] = grad_part
            top = 4 * BLOCK * head
            near[top : top + BLOCK, :] = query_part
            near[top + BLOCK : top + 2 * BLOCK, :] = grad_part
            near[top + 2 * BLOCK : top + 3 * BLOCK, :] = key[0, :, columns]
            near[top + 3 * BLOCK : top + 4 * BLOCK, :] = value[0, :, columns]
            delta = jnp.sum(jnp.transpose(products), axis=0, keepdims=True)
            rows += split_two(lse[owner * share + head]) + split_two(delta)
        rows.append(jnp.zeros((stat_rows - 4 * share, BLOCK), jnp.float32))
        stats = jnp.concatenate(rows, axis=0).astype(jnp.bfloat16)
        far[2 * BLOCK * share : 2 * BLOCK * share + stat_rows, :] = stats
        near[4 * BLOCK * share : 4 * BLOCK * share + stat_rows, :] = stats


def table_kernel(plan, bias, index, count, shift):
    members, share, blocks = plan["members"], plan["share"], plan["blocks"]
    heads = members * share
    me = lax.axis_index("gene")
    mine = me % members
    for place in range(blocks):
        row = me ^ place
        for at in range(members * share):
            shift[place * members * share + at] = UNLISTED

        def listed(slot, carry, place=place, row=row):
            side = index[row * blocks + slot] ^ me

            @pl.when(side < members)
            def _():
                for head in range(share):
                    shift[(place * members + side) * share + head] = LOG2E * bias[
                        (row * heads + mine * share + head) * blocks + slot
                    ]

            return carry

        lax.fori_loop(0, count[row], listed, 0)


def stage_kernel(plan, places, first, last, shift, *refs):
    members, share, scale = plan["members"], plan["share"], plan["scale"]
    count = len(places)
    mine = lax.axis_index("gene") % members
    near, rest = [refs[0].at[mine ^ hop] for hop in range(members)], refs[1:]
    fresh = [place for place in places if place >= members]
    pieces = [near[place] for place in places if place < members] + list(rest[: len(fresh)])
    steps = [(4 if place < members else 2) * BLOCK for place in places]
    rest = rest[len(fresh) :]
    before = None
    if not first:
        before, rest = rest[:2], rest[2:]
    outs, rest = rest[:count], rest[count:]
    if last:
        owned, rest = rest[:members], rest[members:]
    else:
        after, rest = rest[:2], rest[2:]
    weights_low, grads_low, sums = rest
    nt = (((1,), (1,)), ((), ()))
    nn = (((1,), (0,)), ((), ()))
    tn = (((0,), (0,)), ((), ()))
    dot = functools.partial(lax.dot_general, preferred_element_type=jnp.float32)
    stats = [
        piece[step * share : step * share + plan["stat_rows"], :].astype(jnp.float32)
        for piece, step in zip(pieces, steps)
    ]
    wide = 2 if count % 2 == 0 else 1
    total_rows = share * members
    if plan["sum_rows"] > total_rows:
        for at in range(count):
            sums[at, total_rows:, :] = jnp.zeros((plan["sum_rows"] - total_rows, BLOCK), jnp.float32)

    def own(side, head, which):
        top = 4 * BLOCK * head + (2 + which) * BLOCK
        return near[side][top : top + BLOCK, :]

    def rows(at, head, which):
        top = steps[at] * head + which * BLOCK
        return pieces[at][top : top + BLOCK, :]

    for head in range(share):
        for group in range(0, count, wide):
            ats = range(group, group + wide)
            queries = jnp.concatenate([rows(at, head, 0) for at in ats], axis=0)
            grads = jnp.concatenate([rows(at, head, 1) for at in ats], axis=0)
            line = jnp.concatenate([stats[at][4 * head : 4 * head + 4] for at in ats], axis=1)
            saved = (line[0:1] + line[1:2]) * LOG2E
            delta = line[2:3] + line[3:4]
            spot = slice(group * BLOCK, (group + wide) * BLOCK)
            for side in range(members):
                part = slice(side * BLOCK, (side + 1) * BLOCK)
                scores = dot(own(side, head, 0), queries, nt)
                weight_grads = dot(own(side, head, 1), grads, nt)
                shifts = [
                    jnp.full((1, BLOCK), shift[(places[at] * members + side) * share + head])
                    for at in ats
                ]
                offset = jnp.concatenate(shifts, axis=1) - saved
                weights = jnp.exp2(scores * (scale * LOG2E) + offset)
                score_grads = weights * (weight_grads - delta)
                weights_low[part, spot] = weights.astype(jnp.bfloat16)
                grads_low[part, spot] = score_grads.astype(jnp.bfloat16)
                column_sums = jnp.sum(score_grads, axis=0, keepdims=True)
                row = head * members + side
                for at in ats:
                    lanes = slice((at - group) * BLOCK, (at - group + 1) * BLOCK)
                    sums[at, row : row + 1, :] = column_sums[:, lanes]
        keys = jnp.concatenate([own(side, head, 0) for side in range(members)], axis=0)
        queries = jnp.concatenate([rows(at, head, 0) for at in range(count)], axis=0)
        grads = jnp.concatenate([rows(at, head, 1) for at in range(count)], axis=0)
        query_grad = dot(grads_low[...], keys, tn) * scale
        for at in range(count):
            outs[at][head * BLOCK : (head + 1) * BLOCK, :] = query_grad[
                at * BLOCK : (at + 1) * BLOCK
            ].astype(jnp.bfloat16)
        value_grad = dot(weights_low[...], grads, nn)
        key_grad = dot(grads_low[...], queries, nn)
        if before is not None:
            key_grad = key_grad + before[0][head]
            value_grad = value_grad + before[1][head]
        if last:
            key_grad = key_grad * scale
            top = 2 * BLOCK * head
            for side in range(members):
                part = slice(side * BLOCK, (side + 1) * BLOCK)
                owned[side][top : top + BLOCK, :] = key_grad[part].astype(jnp.bfloat16)
                owned[side][top + BLOCK : top + 2 * BLOCK, :] = value_grad[part].astype(jnp.bfloat16)
        else:
            after[0][head] = key_grad
            after[1][head] = value_grad
    lane = lax.broadcasted_iota(jnp.int32, (plan["sum_rows"], BLOCK), 1)
    for at in range(count):
        total = jnp.sum(sums[at], axis=1, keepdims=True)
        high, low = split_two(total)
        middle, low = split_two(low)
        spread = jnp.where(lane == 1, middle, jnp.where(lane == 2, low, 0.0))
        spread = jnp.where(lane == 0, high, spread)
        outs[at][share * BLOCK : share * BLOCK + plan["sum_rows"], :] = spread.astype(jnp.bfloat16)


def bias_kernel(plan, index, *refs):
    blocks, members, share, cells = plan["blocks"], plan["members"], plan["share"], plan["cells"]
    heads, per_cell = members * share, blocks // cells
    pieces, parts = refs[:blocks], refs[blocks : blocks + cells]
    slots, sums, table = refs[blocks + cells :]
    me, cell = lax.axis_index("gene"), lax.axis_index("cell")
    mine = me % members
    for slot in range(blocks):
        slots[index[me * blocks + slot]] = slot
    for hop in range(members):
        owner = mine ^ hop
        for other in range(hop, blocks, members):
            rows = pieces[other][share * BLOCK : share * BLOCK + plan["sum_rows"], :]
            rows = rows.astype(jnp.float32)
            for side in range(members):
                slot = slots[me ^ other ^ side]
                for head in range(share):
                    at = head * members + side
                    sums[pl.ds(slot * heads + owner * share + head, 1), :] = rows[at : at + 1]
    line = jnp.sum(jnp.transpose(sums[...]), axis=0, keepdims=True)
    for slot in range(blocks):
        table[slot : slot + 1, 0:heads] = line[:, slot * heads : (slot + 1) * heads]
    for hop in range(cells):
        for slot in range(per_cell):
            parts[hop][slot : slot + 1, :] = table[pl.ds((cell ^ hop) * per_cell + slot, 1), 0:heads]


def unpack_kernel(plan, *refs):
    blocks, members, share = plan["blocks"], plan["members"], plan["share"]
    head_size = plan["head_size"]
    pieces, owned = refs[:blocks], refs[blocks : blocks + members]
    query_grad, key_grad, value_grad = refs[-3:]
    mine = lax.axis_index("gene") % members
    for hop in range(members):
        start = pl.multiple_of((mine ^ hop) * (share * head_size), head_size)
        for head in range(share):
            columns = pl.ds(start + head * head_size, head_size)
            top = head * BLOCK
            total = pieces[hop][top : top + BLOCK, :].astype(jnp.float32)
            for other in range(members + hop, blocks, members):
                total = total + pieces[other][top : top + BLOCK, :].astype(jnp.float32)
            query_grad[0, :, columns] = total.astype(jnp.bfloat16)
            top = 2 * BLOCK * head
            key_grad[0, :, columns] = owned[hop][top : top + BLOCK, :]
            value_grad[0, :, columns] = owned[hop][top + BLOCK : top + 2 * BLOCK, :]


def call(kernel, outs, scratch=(), smem_in=0, smem_out=False, count=0, limit=VMEM_LIMIT):
    places = [pl.BlockSpec(memory_space=pltpu.SMEM)] * smem_in
    places += [pl.BlockSpec(memory_space=pltpu.VMEM)] * count
    space = pltpu.SMEM if smem_out else pltpu.VMEM
    return pl.pallas_call(
        kernel,
        out_shape=outs,
        in_specs=places,
        out_specs=[pl.BlockSpec(memory_space=space)] * len(outs),
        scratch_shapes=list(scratch),
        compiler_params=pltpu.CompilerParams(vmem_limit_bytes=limit),
    )


def shards(
    query_rows,
    key_rows,
    value_rows,
    output_rows,
    output_grad,
    row_lse,
    block_bias,
    block_index,
    block_count,
):
    row_width = query_rows.shape[2]
    head_count = row_lse.shape[2]
    blocks = block_bias.shape[0]
    members = math.gcd(blocks, head_count)
    share = head_count // members
    head_size = row_width // head_count
    low, full = jnp.bfloat16, jnp.float32
    stat_rows = -(-4 * share // ROW_TILE) * ROW_TILE
    sum_rows = -(-share * members // ROW_TILE) * ROW_TILE
    far_rows = 2 * BLOCK * share + stat_rows
    plan = dict(
        blocks=blocks,
        members=members,
        share=share,
        head_size=head_size,
        stat_rows=stat_rows,
        sum_rows=sum_rows,
        far_rows=far_rows,
        scale=1.0 / math.sqrt(head_size),
    )

    cells = lax.axis_size("cell")
    plan["cells"] = cells
    near_rows = 4 * BLOCK * share + stat_rows
    near_in = jax.ShapeDtypeStruct((members, near_rows, BLOCK), low)
    far_in = jax.ShapeDtypeStruct((far_rows, BLOCK), low)
    sent = call(functools.partial(pack_kernel, plan), [far_in] * members + [near_in], count=6)(
        query_rows, key_rows, value_rows, output_rows, output_grad, jnp.transpose(row_lse, (2, 0, 1))
    )
    groups = [list(range(at, at + members)) for at in range(0, blocks, members)]

    def exchange(array):
        return lax.all_to_all(array, "gene", 0, 0, axis_index_groups=groups)

    def move(array, hop, axis="gene", size=blocks):
        return lax.ppermute(array, axis, [(i, i ^ hop) for i in range(size)])

    far = {hop: move(sent[hop % members], hop) for hop in range(members, blocks)}
    near = exchange(sent[members])
    (table,) = call(
        functools.partial(table_kernel, plan),
        [jax.ShapeDtypeStruct((blocks * members * share,), full)],
        smem_in=3,
        smem_out=True,
    )(block_bias.reshape(-1), block_index.reshape(-1), block_count)
    query_out = jax.ShapeDtypeStruct((share * BLOCK + sum_rows, BLOCK), low)
    partial_out = jax.ShapeDtypeStruct((share, members * BLOCK, BLOCK), full)
    owner_out = jax.ShapeDtypeStruct((2 * BLOCK * share, BLOCK), low)

    def stage(places, first, last, partials):
        count = len(places)
        pieces = [far[place] for place in places if place >= members]
        scratch = pltpu.VMEM((members * BLOCK, count * BLOCK), low)
        made = call(
            functools.partial(stage_kernel, plan, places, first, last),
            [query_out] * count + ([owner_out] * members if last else [partial_out] * 2),
            scratch=[scratch, scratch, pltpu.VMEM((count, sum_rows, BLOCK), full)],
            smem_in=1,
            count=1 + len(pieces) + len(partials),
            limit=STAGE_LIMIT,
        )(table, near, *pieces, *partials)
        return made[:count], made[count:]

    queries, partials, begin = [], [], 0
    for end in (members + (blocks - members) // 2, blocks):
        places = tuple(range(begin, end))
        made, partials = stage(places, begin == 0, end == blocks, partials)
        queries += [move(piece, place) if place else piece for piece, place in zip(made, places)]
        begin = end
    owned = [partials[0]] + [move(partials[hop], hop) for hop in range(1, members)]
    whole = jax.ShapeDtypeStruct((1, BLOCK, row_width), low)
    part_out = jax.ShapeDtypeStruct((blocks // cells, head_count), full)
    parts = call(
        functools.partial(bias_kernel, plan),
        [part_out] * cells,
        scratch=[
            pltpu.SMEM((blocks,), jnp.int32),
            pltpu.VMEM((head_count * blocks, BLOCK), full),
            pltpu.VMEM((blocks, BLOCK), full),
        ],
        smem_in=1,
        count=blocks,
        limit=STAGE_LIMIT,
    )(block_index.reshape(-1), *queries)
    query_grad, key_grad, value_grad = call(
        functools.partial(unpack_kernel, plan),
        [whole] * 3,
        count=blocks + members + 1,
        limit=STAGE_LIMIT,
    )(*queries, *owned, parts[0])
    parts = [parts[0]] + [move(parts[hop], hop, "cell", cells) for hop in range(1, cells)]
    bias_grad = jnp.transpose(functools.reduce(jnp.add, parts))[None]
    return (query_grad, key_grad, value_grad, bias_grad)


def solution(mesh):
    rows = P("cell", "gene", None)
    in_specs = (rows,) * 6 + (P(),) * 3
    out_specs = (rows, rows, rows, P("gene", None, "cell"))
    return jax.shard_map(shards, mesh=mesh, in_specs=in_specs, out_specs=out_specs, check_vma=False)
```

```python
import functools
import math

import jax
import jax.numpy as jnp
from jax import lax
from jax.experimental import pallas as pl
from jax.experimental.pallas import tpu as pltpu
from jax.sharding import PartitionSpec as P

BLOCK = 128
ROW_TILE = 16
VMEM_LIMIT = 60 * 1024 * 1024
STAGE_LIMIT = 40 * 1024 * 1024
LOG2E = math.log2(math.e)
UNLISTED = -1e30


def split_two(row):
    high = row.astype(jnp.bfloat16).astype(jnp.float32)
    return [high, row - high]


def pack_kernel(plan, query, key, value, output, grad, lse, *outs):
    members, share, head_size = plan["members"], plan["share"], plan["head_size"]
    width, stat_rows = share * head_size, plan["stat_rows"]
    mine = lax.axis_index("gene") % members
    for hop in range(members):
        owner = mine ^ hop
        near, far = outs[members].at[owner], outs[hop]
        start = pl.multiple_of(owner * width, head_size)
        rows = []
        for head in range(share):
            columns = pl.ds(start + head * head_size, head_size)
            query_part, grad_part = query[0, :, columns], grad[0, :, columns]
            products = grad_part.astype(jnp.float32) * output[0, :, columns].astype(jnp.float32)
            top = 2 * BLOCK * head
            far[top : top + BLOCK, :] = query_part
            far[top + BLOCK : top + 2 * BLOCK, :] = grad_part
            top = 4 * BLOCK * head
            near[top : top + BLOCK, :] = query_part
            near[top + BLOCK : top + 2 * BLOCK, :] = grad_part
            near[top + 2 * BLOCK : top + 3 * BLOCK, :] = key[0, :, columns]
            near[top + 3 * BLOCK : top + 4 * BLOCK, :] = value[0, :, columns]
            delta = jnp.sum(jnp.transpose(products), axis=0, keepdims=True)
            rows += split_two(lse[owner * share + head]) + split_two(delta)
        rows.append(jnp.zeros((stat_rows - 4 * share, BLOCK), jnp.float32))
        stats = jnp.concatenate(rows, axis=0).astype(jnp.bfloat16)
        far[2 * BLOCK * share : 2 * BLOCK * share + stat_rows, :] = stats
        near[4 * BLOCK * share : 4 * BLOCK * share + stat_rows, :] = stats


def table_kernel(plan, bias, index, count, shift):
    members, share, blocks = plan["members"], plan["share"], plan["blocks"]
    heads = members * share
    me = lax.axis_index("gene")
    mine = me % members
    for place in range(blocks):
        row = me ^ place
        for at in range(members * share):
            shift[place * members * share + at] = UNLISTED

        def listed(slot, carry, place=place, row=row):
            side = index[row * blocks + slot] ^ me

            @pl.when(side < members)
            def _():
                for head in range(share):
                    shift[(place * members + side) * share + head] = LOG2E * bias[
                        (row * heads + mine * share + head) * blocks + slot
                    ]

            return carry

        lax.fori_loop(0, count[row], listed, 0)


def stage_kernel(plan, places, first, last, shift, *refs):
    members, share, scale = plan["members"], plan["share"], plan["scale"]
    count = len(places)
    mine = lax.axis_index("gene") % members
    near, rest = [refs[0].at[mine ^ hop] for hop in range(members)], refs[1:]
    fresh = [place for place in places if place >= members]
    pieces = [near[place] for place in places if place < members] + list(rest[: len(fresh)])
    steps = [(4 if place < members else 2) * BLOCK for place in places]
    rest = rest[len(fresh) :]
    before = None
    if not first:
        before, rest = rest[:2], rest[2:]
    outs, rest = rest[:count], rest[count:]
    if last:
        owned, rest = rest[:members], rest[members:]
    else:
        after, rest = rest[:2], rest[2:]
    weights_low, grads_low, sums = rest
    nt = (((1,), (1,)), ((), ()))
    nn = (((1,), (0,)), ((), ()))
    tn = (((0,), (0,)), ((), ()))
    dot = functools.partial(lax.dot_general, preferred_element_type=jnp.float32)
    stats = [
        piece[step * share : step * share + plan["stat_rows"], :].astype(jnp.float32)
        for piece, step in zip(pieces, steps)
    ]
    wide = 2 if count % 2 == 0 else 1
    total_rows = share * members
    if plan["sum_rows"] > total_rows:
        for at in range(count):
            sums[at, total_rows:, :] = jnp.zeros((plan["sum_rows"] - total_rows, BLOCK), jnp.float32)

    def own(side, head, which):
        top = 4 * BLOCK * head + (2 + which) * BLOCK
        return near[side][top : top + BLOCK, :]

    def rows(at, head, which):
        top = steps[at] * head + which * BLOCK
        return pieces[at][top : top + BLOCK, :]

    for head in range(share):
        for group in range(0, count, wide):
            ats = range(group, group + wide)
            queries = jnp.concatenate([rows(at, head, 0) for at in ats], axis=0)
            grads = jnp.concatenate([rows(at, head, 1) for at in ats], axis=0)
            line = jnp.concatenate([stats[at][4 * head : 4 * head + 4] for at in ats], axis=1)
            saved = (line[0:1] + line[1:2]) * LOG2E
            delta = line[2:3] + line[3:4]
            spot = slice(group * BLOCK, (group + wide) * BLOCK)
            for side in range(members):
                part = slice(side * BLOCK, (side + 1) * BLOCK)
                scores = dot(own(side, head, 0), queries, nt)
                weight_grads = dot(own(side, head, 1), grads, nt)
                shifts = [
                    jnp.full((1, BLOCK), shift[(places[at] * members + side) * share + head])
                    for at in ats
                ]
                offset = jnp.concatenate(shifts, axis=1) - saved
                weights = jnp.exp2(scores * (scale * LOG2E) + offset)
                score_grads = weights * (weight_grads - delta)
                weights_low[part, spot] = weights.astype(jnp.bfloat16)
                grads_low[part, spot] = score_grads.astype(jnp.bfloat16)
                column_sums = jnp.sum(score_grads, axis=0, keepdims=True)
                row = head * members + side
                for at in ats:
                    lanes = slice((at - group) * BLOCK, (at - group + 1) * BLOCK)
                    sums[at, row : row + 1, :] = column_sums[:, lanes]
        keys = jnp.concatenate([own(side, head, 0) for side in range(members)], axis=0)
        queries = jnp.concatenate([rows(at, head, 0) for at in range(count)], axis=0)
        grads = jnp.concatenate([rows(at, head, 1) for at in range(count)], axis=0)
        query_grad = dot(grads_low[...], keys, tn) * scale
        for at in range(count):
            outs[at][head * BLOCK : (head + 1) * BLOCK, :] = query_grad[
                at * BLOCK : (at + 1) * BLOCK
            ].astype(jnp.bfloat16)
        value_grad = dot(weights_low[...], grads, nn)
        key_grad = dot(grads_low[...], queries, nn)
        if before is not None:
            key_grad = key_grad + before[0][head]
            value_grad = value_grad + before[1][head]
        if last:
            key_grad = key_grad * scale
            top = 2 * BLOCK * head
            for side in range(members):
                part = slice(side * BLOCK, (side + 1) * BLOCK)
                owned[side][top : top + BLOCK, :] = key_grad[part].astype(jnp.bfloat16)
                owned[side][top + BLOCK : top + 2 * BLOCK, :] = value_grad[part].astype(jnp.bfloat16)
        else:
            after[0][head] = key_grad
            after[1][head] = value_grad
    lane = lax.broadcasted_iota(jnp.int32, (plan["sum_rows"], BLOCK), 1)
    for at in range(count):
        total = jnp.sum(sums[at], axis=1, keepdims=True)
        high, low = split_two(total)
        middle, low = split_two(low)
        spread = jnp.where(lane == 1, middle, jnp.where(lane == 2, low, 0.0))
        spread = jnp.where(lane == 0, high, spread)
        outs[at][share * BLOCK : share * BLOCK + plan["sum_rows"], :] = spread.astype(jnp.bfloat16)


def bias_kernel(plan, index, *refs):
    blocks, members, share, cells = plan["blocks"], plan["members"], plan["share"], plan["cells"]
    heads, per_cell = members * share, blocks // cells
    pieces, parts = refs[:blocks], refs[blocks : blocks + cells]
    slots, sums, table = refs[blocks + cells :]
    me, cell = lax.axis_index("gene"), lax.axis_index("cell")
    mine = me % members
    for slot in range(blocks):
        slots[index[me * blocks + slot]] = slot
    for hop in range(members):
        owner = mine ^ hop
        for other in range(hop, blocks, members):
            rows = pieces[other][share * BLOCK : share * BLOCK + plan["sum_rows"], :]
            rows = rows.astype(jnp.float32)
            for side in range(members):
                slot = slots[me ^ other ^ side]
                for head in range(share):
                    at = head * members + side
                    sums[pl.ds(slot * heads + owner * share + head, 1), :] = rows[at : at + 1]
    line = jnp.sum(jnp.transpose(sums[...]), axis=0, keepdims=True)
    for slot in range(blocks):
        table[slot : slot + 1, 0:heads] = line[:, slot * heads : (slot + 1) * heads]
    for hop in range(cells):
        for slot in range(per_cell):
            parts[hop][slot : slot + 1, :] = table[pl.ds((cell ^ hop) * per_cell + slot, 1), 0:heads]


def unpack_kernel(plan, *refs):
    blocks, members, share = plan["blocks"], plan["members"], plan["share"]
    head_size = plan["head_size"]
    pieces, owned = refs[:blocks], refs[blocks : blocks + members]
    query_grad, key_grad, value_grad, passed = refs[-4:]
    passed[...] = refs[blocks + members][...]
    mine = lax.axis_index("gene") % members
    for hop in range(members):
        start = pl.multiple_of((mine ^ hop) * (share * head_size), head_size)
        for head in range(share):
            columns = pl.ds(start + head * head_size, head_size)
            top = head * BLOCK
            total = pieces[hop][top : top + BLOCK, :].astype(jnp.float32)
            for other in range(members + hop, blocks, members):
                total = total + pieces[other][top : top + BLOCK, :].astype(jnp.float32)
            query_grad[0, :, columns] = total.astype(jnp.bfloat16)
            top = 2 * BLOCK * head
            key_grad[0, :, columns] = owned[hop][top : top + BLOCK, :]
            value_grad[0, :, columns] = owned[hop][top + BLOCK : top + 2 * BLOCK, :]


def call(kernel, outs, scratch=(), smem_in=0, smem_out=False, count=0, limit=VMEM_LIMIT, flops=None):
    places = [pl.BlockSpec(memory_space=pltpu.SMEM)] * smem_in
    places += [pl.BlockSpec(memory_space=pltpu.VMEM)] * count
    space = pltpu.SMEM if smem_out else pltpu.VMEM
    return pl.pallas_call(
        kernel,
        out_shape=outs,
        in_specs=places,
        out_specs=[pl.BlockSpec(memory_space=space)] * len(outs),
        scratch_shapes=list(scratch),
        compiler_params=pltpu.CompilerParams(vmem_limit_bytes=limit),
        cost_estimate=flops and pl.CostEstimate(flops=flops, bytes_accessed=0, transcendentals=0),
    )


def shards(
    query_rows,
    key_rows,
    value_rows,
    output_rows,
    output_grad,
    row_lse,
    block_bias,
    block_index,
    block_count,
):
    row_width = query_rows.shape[2]
    head_count = row_lse.shape[2]
    blocks = block_bias.shape[0]
    members = math.gcd(blocks, head_count)
    share = head_count // members
    head_size = row_width // head_count
    low, full = jnp.bfloat16, jnp.float32
    stat_rows = -(-4 * share // ROW_TILE) * ROW_TILE
    sum_rows = -(-share * members // ROW_TILE) * ROW_TILE
    far_rows = 2 * BLOCK * share + stat_rows
    plan = dict(
        blocks=blocks,
        members=members,
        share=share,
        head_size=head_size,
        stat_rows=stat_rows,
        sum_rows=sum_rows,
        far_rows=far_rows,
        scale=1.0 / math.sqrt(head_size),
    )

    cells = lax.axis_size("cell")
    plan["cells"] = cells
    near_rows = 4 * BLOCK * share + stat_rows
    near_in = jax.ShapeDtypeStruct((members, near_rows, BLOCK), low)
    far_in = jax.ShapeDtypeStruct((far_rows, BLOCK), low)
    sent = call(functools.partial(pack_kernel, plan), [far_in] * members + [near_in], count=6)(
        query_rows, key_rows, value_rows, output_rows, output_grad, jnp.transpose(row_lse, (2, 0, 1))
    )
    groups = [list(range(at, at + members)) for at in range(0, blocks, members)]

    def exchange(array):
        return lax.all_to_all(array, "gene", 0, 0, axis_index_groups=groups)

    def move(array, hop, axis="gene", size=blocks):
        return lax.ppermute(array, axis, [(i, i ^ hop) for i in range(size)])

    far = {hop: move(sent[hop % members], hop) for hop in range(members, blocks)}
    near = exchange(sent[members])
    (table,) = call(
        functools.partial(table_kernel, plan),
        [jax.ShapeDtypeStruct((blocks * members * share,), full)],
        smem_in=3,
        smem_out=True,
    )(block_bias.reshape(-1), block_index.reshape(-1), block_count)
    query_out = jax.ShapeDtypeStruct((share * BLOCK + sum_rows, BLOCK), low)
    partial_out = jax.ShapeDtypeStruct((share, members * BLOCK, BLOCK), full)
    owner_out = jax.ShapeDtypeStruct((2 * BLOCK * share, BLOCK), low)

    def stage(places, first, last, partials):
        count = len(places)
        pieces = [far[place] for place in places if place >= members]
        scratch = pltpu.VMEM((members * BLOCK, count * BLOCK), low)
        made = call(
            functools.partial(stage_kernel, plan, places, first, last),
            [query_out] * count + ([owner_out] * members if last else [partial_out] * 2),
            scratch=[scratch, scratch, pltpu.VMEM((count, sum_rows, BLOCK), full)],
            smem_in=1,
            count=1 + len(pieces) + len(partials),
            limit=STAGE_LIMIT,
        )(table, near, *pieces, *partials)
        return made[:count], made[count:]

    queries, partials, begin = [], [], 0
    for end in (members + (blocks - members) // 2, blocks):
        places = tuple(range(begin, end))
        made, partials = stage(places, begin == 0, end == blocks, partials)
        queries += [move(piece, place) if place else piece for piece, place in zip(made, places)]
        begin = end
    owned = [partials[0]] + [move(partials[hop], hop) for hop in range(1, members)]
    whole = jax.ShapeDtypeStruct((1, BLOCK, row_width), low)
    part_out = jax.ShapeDtypeStruct((blocks // cells, head_count), full)
    parts = call(
        functools.partial(bias_kernel, plan),
        [part_out] * cells,
        scratch=[
            pltpu.SMEM((blocks,), jnp.int32),
            pltpu.VMEM((head_count * blocks, BLOCK), full),
            pltpu.VMEM((blocks, BLOCK), full),
        ],
        smem_in=1,
        count=blocks,
        limit=STAGE_LIMIT,
        flops=40000000000,
    )(block_index.reshape(-1), *queries)
    query_grad, key_grad, value_grad, own_part = call(
        functools.partial(unpack_kernel, plan),
        [whole] * 3 + [part_out],
        count=blocks + members + 1,
        limit=STAGE_LIMIT,
    )(*queries, *owned, parts[0])
    parts = [own_part] + [move(parts[hop], hop, "cell", cells) for hop in range(1, cells)]
    bias_grad = jnp.transpose(functools.reduce(jnp.add, parts))[None]
    return (query_grad, key_grad, value_grad, bias_grad)


def solution(mesh):
    rows = P("cell", "gene", None)
    in_specs = (rows,) * 6 + (P(),) * 3
    out_specs = (rows, rows, rows, P("gene", None, "cell"))
    return jax.shard_map(shards, mesh=mesh, in_specs=in_specs, out_specs=out_specs, check_vma=False)
```

```python
import functools
import math

import jax
import jax.numpy as jnp
from jax import lax
from jax.experimental import pallas as pl
from jax.experimental.pallas import tpu as pltpu
from jax.sharding import PartitionSpec as P

BLOCK = 128
ROW_TILE = 16
VMEM_LIMIT = 60 * 1024 * 1024
STAGE_LIMIT = 40 * 1024 * 1024
LOG2E = math.log2(math.e)
UNLISTED = -1e30


def split_two(row):
    high = row.astype(jnp.bfloat16).astype(jnp.float32)
    return [high, row - high]


def pack_kernel(plan, query, key, value, output, grad, lse, *outs):
    members, share, head_size = plan["members"], plan["share"], plan["head_size"]
    width, stat_rows = share * head_size, plan["stat_rows"]
    mine = lax.axis_index("gene") % members
    for hop in range(members):
        owner = mine ^ hop
        near, far = outs[members].at[owner], outs[hop]
        start = pl.multiple_of(owner * width, head_size)
        rows = []
        for head in range(share):
            columns = pl.ds(start + head * head_size, head_size)
            query_part, grad_part = query[0, :, columns], grad[0, :, columns]
            products = grad_part.astype(jnp.float32) * output[0, :, columns].astype(jnp.float32)
            top = 2 * BLOCK * head
            far[top : top + BLOCK, :] = query_part
            far[top + BLOCK : top + 2 * BLOCK, :] = grad_part
            top = 4 * BLOCK * head
            near[top : top + BLOCK, :] = query_part
            near[top + BLOCK : top + 2 * BLOCK, :] = grad_part
            near[top + 2 * BLOCK : top + 3 * BLOCK, :] = key[0, :, columns]
            near[top + 3 * BLOCK : top + 4 * BLOCK, :] = value[0, :, columns]
            delta = jnp.sum(jnp.transpose(products), axis=0, keepdims=True)
            rows += split_two(lse[owner * share + head]) + split_two(delta)
        rows.append(jnp.zeros((stat_rows - 4 * share, BLOCK), jnp.float32))
        stats = jnp.concatenate(rows, axis=0).astype(jnp.bfloat16)
        far[2 * BLOCK * share : 2 * BLOCK * share + stat_rows, :] = stats
        near[4 * BLOCK * share : 4 * BLOCK * share + stat_rows, :] = stats


def table_kernel(plan, bias, index, count, shift):
    members, share, blocks = plan["members"], plan["share"], plan["blocks"]
    heads = members * share
    me = lax.axis_index("gene")
    mine = me % members
    for place in range(blocks):
        row = me ^ place
        for at in range(members * share):
            shift[place * members * share + at] = UNLISTED

        def listed(slot, carry, place=place, row=row):
            side = index[row * blocks + slot] ^ me

            @pl.when(side < members)
            def _():
                for head in range(share):
                    shift[(place * members + side) * share + head] = LOG2E * bias[
                        (row * heads + mine * share + head) * blocks + slot
                    ]

            return carry

        lax.fori_loop(0, count[row], listed, 0)


def stage_kernel(plan, places, first, last, shift, *refs):
    members, share, scale = plan["members"], plan["share"], plan["scale"]
    count = len(places)
    mine = lax.axis_index("gene") % members
    near, rest = [refs[0].at[mine ^ hop] for hop in range(members)], refs[1:]
    fresh = [place for place in places if place >= members]
    pieces = [near[place] for place in places if place < members] + list(rest[: len(fresh)])
    steps = [(4 if place < members else 2) * BLOCK for place in places]
    rest = rest[len(fresh) :]
    before = None
    if not first:
        before, rest = rest[:2], rest[2:]
    outs, rest = rest[:count], rest[count:]
    if last:
        owned, rest = rest[:members], rest[members:]
    else:
        after, rest = rest[:2], rest[2:]
    weights_low, grads_low, sums = rest
    nt = (((1,), (1,)), ((), ()))
    nn = (((1,), (0,)), ((), ()))
    tn = (((0,), (0,)), ((), ()))
    dot = functools.partial(lax.dot_general, preferred_element_type=jnp.float32)
    stats = [
        piece[step * share : step * share + plan["stat_rows"], :].astype(jnp.float32)
        for piece, step in zip(pieces, steps)
    ]
    wide = 2 if count % 2 == 0 else 1
    total_rows = share * members
    if plan["sum_rows"] > total_rows:
        for at in range(count):
            sums[at, total_rows:, :] = jnp.zeros((plan["sum_rows"] - total_rows, BLOCK), jnp.float32)

    def own(side, head, which):
        top = 4 * BLOCK * head + (2 + which) * BLOCK
        return near[side][top : top + BLOCK, :]

    def rows(at, head, which):
        top = steps[at] * head + which * BLOCK
        return pieces[at][top : top + BLOCK, :]

    for head in range(share):
        for group in range(0, count, wide):
            ats = range(group, group + wide)
            queries = jnp.concatenate([rows(at, head, 0) for at in ats], axis=0)
            grads = jnp.concatenate([rows(at, head, 1) for at in ats], axis=0)
            line = jnp.concatenate([stats[at][4 * head : 4 * head + 4] for at in ats], axis=1)
            saved = (line[0:1] + line[1:2]) * LOG2E
            delta = line[2:3] + line[3:4]
            spot = slice(group * BLOCK, (group + wide) * BLOCK)
            for side in range(members):
                part = slice(side * BLOCK, (side + 1) * BLOCK)
                scores = dot(own(side, head, 0), queries, nt)
                weight_grads = dot(own(side, head, 1), grads, nt)
                shifts = [
                    jnp.full((1, BLOCK), shift[(places[at] * members + side) * share + head])
                    for at in ats
                ]
                offset = jnp.concatenate(shifts, axis=1) - saved
                weights = jnp.exp2(scores * (scale * LOG2E) + offset)
                score_grads = weights * (weight_grads - delta)
                weights_low[part, spot] = weights.astype(jnp.bfloat16)
                grads_low[part, spot] = score_grads.astype(jnp.bfloat16)
                column_sums = jnp.sum(score_grads, axis=0, keepdims=True)
                row = head * members + side
                for at in ats:
                    lanes = slice((at - group) * BLOCK, (at - group + 1) * BLOCK)
                    sums[at, row : row + 1, :] = column_sums[:, lanes]
        keys = jnp.concatenate([own(side, head, 0) for side in range(members)], axis=0)
        queries = jnp.concatenate([rows(at, head, 0) for at in range(count)], axis=0)
        grads = jnp.concatenate([rows(at, head, 1) for at in range(count)], axis=0)
        query_grad = dot(grads_low[...], keys, tn) * scale
        for at in range(count):
            outs[at][head * BLOCK : (head + 1) * BLOCK, :] = query_grad[
                at * BLOCK : (at + 1) * BLOCK
            ].astype(jnp.bfloat16)
        value_grad = dot(weights_low[...], grads, nn)
        key_grad = dot(grads_low[...], queries, nn)
        if before is not None:
            key_grad = key_grad + before[0][head]
            value_grad = value_grad + before[1][head]
        if last:
            key_grad = key_grad * scale
            top = 2 * BLOCK * head
            for side in range(members):
                part = slice(side * BLOCK, (side + 1) * BLOCK)
                owned[side][top : top + BLOCK, :] = key_grad[part].astype(jnp.bfloat16)
                owned[side][top + BLOCK : top + 2 * BLOCK, :] = value_grad[part].astype(jnp.bfloat16)
        else:
            after[0][head] = key_grad
            after[1][head] = value_grad
    lane = lax.broadcasted_iota(jnp.int32, (plan["sum_rows"], BLOCK), 1)
    for at in range(count):
        total = jnp.sum(sums[at], axis=1, keepdims=True)
        high, low = split_two(total)
        middle, low = split_two(low)
        spread = jnp.where(lane == 1, middle, jnp.where(lane == 2, low, 0.0))
        spread = jnp.where(lane == 0, high, spread)
        outs[at][share * BLOCK : share * BLOCK + plan["sum_rows"], :] = spread.astype(jnp.bfloat16)


def bias_kernel(plan, index, *refs):
    blocks, members, share, cells = plan["blocks"], plan["members"], plan["share"], plan["cells"]
    heads, per_cell = members * share, blocks // cells
    pieces, parts = refs[:blocks], refs[blocks : blocks + cells]
    slots, sums, table = refs[blocks + cells :]
    me, cell = lax.axis_index("gene"), lax.axis_index("cell")
    mine = me % members
    for slot in range(blocks):
        slots[index[me * blocks + slot]] = slot
    for hop in range(members):
        owner = mine ^ hop
        for other in range(hop, blocks, members):
            rows = pieces[other][share * BLOCK : share * BLOCK + plan["sum_rows"], :]
            rows = rows.astype(jnp.float32)
            for side in range(members):
                slot = slots[me ^ other ^ side]
                for head in range(share):
                    at = head * members + side
                    sums[pl.ds(slot * heads + owner * share + head, 1), :] = rows[at : at + 1]
    line = jnp.sum(jnp.transpose(sums[...]), axis=0, keepdims=True)
    for slot in range(blocks):
        table[slot : slot + 1, 0:heads] = line[:, slot * heads : (slot + 1) * heads]
    for hop in range(cells):
        for slot in range(per_cell):
            parts[hop][slot : slot + 1, :] = table[pl.ds((cell ^ hop) * per_cell + slot, 1), 0:heads]


def unpack_kernel(plan, *refs):
    blocks, members, share = plan["blocks"], plan["members"], plan["share"]
    head_size = plan["head_size"]
    pieces, owned = refs[:blocks], refs[blocks : blocks + members]
    query_grad, key_grad, value_grad, passed = refs[-4:]
    passed[...] = refs[blocks + members][...]
    mine = lax.axis_index("gene") % members
    for hop in range(members):
        start = pl.multiple_of((mine ^ hop) * (share * head_size), head_size)
        for head in range(share):
            columns = pl.ds(start + head * head_size, head_size)
            top = head * BLOCK
            total = pieces[hop][top : top + BLOCK, :].astype(jnp.float32)
            for other in range(members + hop, blocks, members):
                total = total + pieces[other][top : top + BLOCK, :].astype(jnp.float32)
            query_grad[0, :, columns] = total.astype(jnp.bfloat16)
            top = 2 * BLOCK * head
            key_grad[0, :, columns] = owned[hop][top : top + BLOCK, :]
            value_grad[0, :, columns] = owned[hop][top + BLOCK : top + 2 * BLOCK, :]


def call(kernel, outs, scratch=(), smem_in=0, smem_out=False, count=0, limit=VMEM_LIMIT, flops=None):
    places = [pl.BlockSpec(memory_space=pltpu.SMEM)] * smem_in
    places += [pl.BlockSpec(memory_space=pltpu.VMEM)] * count
    space = pltpu.SMEM if smem_out else pltpu.VMEM
    return pl.pallas_call(
        kernel,
        out_shape=outs,
        in_specs=places,
        out_specs=[pl.BlockSpec(memory_space=space)] * len(outs),
        scratch_shapes=list(scratch),
        compiler_params=pltpu.CompilerParams(vmem_limit_bytes=limit),
        cost_estimate=flops and pl.CostEstimate(flops=flops, bytes_accessed=0, transcendentals=0),
    )


def shards(
    query_rows,
    key_rows,
    value_rows,
    output_rows,
    output_grad,
    row_lse,
    block_bias,
    block_index,
    block_count,
):
    row_width = query_rows.shape[2]
    head_count = row_lse.shape[2]
    blocks = block_bias.shape[0]
    members = math.gcd(blocks, head_count)
    share = head_count // members
    head_size = row_width // head_count
    low, full = jnp.bfloat16, jnp.float32
    stat_rows = -(-4 * share // ROW_TILE) * ROW_TILE
    sum_rows = -(-share * members // ROW_TILE) * ROW_TILE
    far_rows = 2 * BLOCK * share + stat_rows
    plan = dict(
        blocks=blocks,
        members=members,
        share=share,
        head_size=head_size,
        stat_rows=stat_rows,
        sum_rows=sum_rows,
        far_rows=far_rows,
        scale=1.0 / math.sqrt(head_size),
    )

    cells = lax.axis_size("cell")
    plan["cells"] = cells
    near_rows = 4 * BLOCK * share + stat_rows
    near_in = jax.ShapeDtypeStruct((members, near_rows, BLOCK), low)
    far_in = jax.ShapeDtypeStruct((far_rows, BLOCK), low)
    sent = call(functools.partial(pack_kernel, plan), [far_in] * members + [near_in], count=6)(
        query_rows, key_rows, value_rows, output_rows, output_grad, jnp.transpose(row_lse, (2, 0, 1))
    )
    groups = [list(range(at, at + members)) for at in range(0, blocks, members)]

    def exchange(array):
        return lax.all_to_all(array, "gene", 0, 0, axis_index_groups=groups)

    def move(array, hop, axis="gene", size=blocks):
        return lax.ppermute(array, axis, [(i, i ^ hop) for i in range(size)])

    far = {hop: move(sent[hop % members], hop) for hop in range(members, blocks)}
    near = exchange(sent[members])
    (table,) = call(
        functools.partial(table_kernel, plan),
        [jax.ShapeDtypeStruct((blocks * members * share,), full)],
        smem_in=3,
        smem_out=True,
    )(block_bias.reshape(-1), block_index.reshape(-1), block_count)
    query_out = jax.ShapeDtypeStruct((share * BLOCK + sum_rows, BLOCK), low)
    partial_out = jax.ShapeDtypeStruct((share, members * BLOCK, BLOCK), full)
    owner_out = jax.ShapeDtypeStruct((2 * BLOCK * share, BLOCK), low)

    def stage(places, first, last, partials):
        count = len(places)
        pieces = [far[place] for place in places if place >= members]
        scratch = pltpu.VMEM((members * BLOCK, count * BLOCK), low)
        made = call(
            functools.partial(stage_kernel, plan, places, first, last),
            [query_out] * count + ([owner_out] * members if last else [partial_out] * 2),
            scratch=[scratch, scratch, pltpu.VMEM((count, sum_rows, BLOCK), full)],
            smem_in=1,
            count=1 + len(pieces) + len(partials),
            limit=STAGE_LIMIT,
        )(table, near, *pieces, *partials)
        return made[:count], made[count:]

    queries, partials, begin = [], [], 0
    for end in (members, blocks):
        places = tuple(range(begin, end))
        made, partials = stage(places, begin == 0, end == blocks, partials)
        queries += [move(piece, place) if place else piece for piece, place in zip(made, places)]
        begin = end
    owned = [partials[0]] + [move(partials[hop], hop) for hop in range(1, members)]
    whole = jax.ShapeDtypeStruct((1, BLOCK, row_width), low)
    part_out = jax.ShapeDtypeStruct((blocks // cells, head_count), full)
    parts = call(
        functools.partial(bias_kernel, plan),
        [part_out] * cells,
        scratch=[
            pltpu.SMEM((blocks,), jnp.int32),
            pltpu.VMEM((head_count * blocks, BLOCK), full),
            pltpu.VMEM((blocks, BLOCK), full),
        ],
        smem_in=1,
        count=blocks,
        limit=STAGE_LIMIT,
        flops=40000000000,
    )(block_index.reshape(-1), *queries)
    query_grad, key_grad, value_grad, own_part = call(
        functools.partial(unpack_kernel, plan),
        [whole] * 3 + [part_out],
        count=blocks + members + 1,
        limit=STAGE_LIMIT,
    )(*queries, *owned, parts[0])
    parts = [own_part] + [move(parts[hop], hop, "cell", cells) for hop in range(1, cells)]
    bias_grad = jnp.transpose(functools.reduce(jnp.add, parts))[None]
    return (query_grad, key_grad, value_grad, bias_grad)


def solution(mesh):
    rows = P("cell", "gene", None)
    in_specs = (rows,) * 6 + (P(),) * 3
    out_specs = (rows, rows, rows, P("gene", None, "cell"))
    return jax.shard_map(shards, mesh=mesh, in_specs=in_specs, out_specs=out_specs, check_vma=False)
```

```python
import functools
import math

import jax
import jax.numpy as jnp
from jax import lax
from jax.experimental import pallas as pl
from jax.experimental.pallas import tpu as pltpu
from jax.sharding import PartitionSpec as P

BLOCK = 128
ROW_TILE = 16
VMEM_LIMIT = 60 * 1024 * 1024
STAGE_LIMIT = 40 * 1024 * 1024
LOG2E = math.log2(math.e)
UNLISTED = -1e30


def split_two(row):
    high = row.astype(jnp.bfloat16).astype(jnp.float32)
    return [high, row - high]


def pack_kernel(plan, query, key, value, output, grad, lse, *outs):
    members, share, head_size = plan["members"], plan["share"], plan["head_size"]
    width, stat_rows = share * head_size, plan["stat_rows"]
    mine = lax.axis_index("gene") % members
    for hop in range(members):
        owner = mine ^ hop
        near, far = outs[hop], outs[members + hop]
        start = pl.multiple_of(owner * width, head_size)
        rows = []
        for head in range(share):
            columns = pl.ds(start + head * head_size, head_size)
            query_part, grad_part = query[0, :, columns], grad[0, :, columns]
            products = grad_part.astype(jnp.float32) * output[0, :, columns].astype(jnp.float32)
            top = 2 * BLOCK * head
            far[top : top + BLOCK, :] = query_part
            far[top + BLOCK : top + 2 * BLOCK, :] = grad_part
            top = 4 * BLOCK * head
            near[top : top + BLOCK, :] = query_part
            near[top + BLOCK : top + 2 * BLOCK, :] = grad_part
            near[top + 2 * BLOCK : top + 3 * BLOCK, :] = key[0, :, columns]
            near[top + 3 * BLOCK : top + 4 * BLOCK, :] = value[0, :, columns]
            delta = jnp.sum(jnp.transpose(products), axis=0, keepdims=True)
            rows += split_two(lse[owner * share + head]) + split_two(delta)
        rows.append(jnp.zeros((stat_rows - 4 * share, BLOCK), jnp.float32))
        stats = jnp.concatenate(rows, axis=0).astype(jnp.bfloat16)
        far[2 * BLOCK * share : 2 * BLOCK * share + stat_rows, :] = stats
        near[4 * BLOCK * share : 4 * BLOCK * share + stat_rows, :] = stats


def table_kernel(plan, bias, index, count, shift):
    members, share, blocks = plan["members"], plan["share"], plan["blocks"]
    heads = members * share
    me = lax.axis_index("gene")
    mine = me % members
    for place in range(blocks):
        row = me ^ place
        for at in range(members * share):
            shift[place * members * share + at] = UNLISTED

        def listed(slot, carry, place=place, row=row):
            side = index[row * blocks + slot] ^ me

            @pl.when(side < members)
            def _():
                for head in range(share):
                    shift[(place * members + side) * share + head] = LOG2E * bias[
                        (row * heads + mine * share + head) * blocks + slot
                    ]

            return carry

        lax.fori_loop(0, count[row], listed, 0)


def stage_kernel(plan, places, first, last, shift, *refs):
    members, share, scale = plan["members"], plan["share"], plan["scale"]
    count = len(places)
    near, rest = refs[:members], refs[members:]
    fresh = [place for place in places if place >= members]
    pieces = [near[place] for place in places if place < members] + list(rest[: len(fresh)])
    steps = [(4 if place < members else 2) * BLOCK for place in places]
    rest = rest[len(fresh) :]
    before = None
    if not first:
        before, rest = rest[:2], rest[2:]
    outs, rest = rest[:count], rest[count:]
    if last:
        owned, rest = rest[:members], rest[members:]
    else:
        after, rest = rest[:2], rest[2:]
    weights_low, grads_low, sums = rest
    nt = (((1,), (1,)), ((), ()))
    nn = (((1,), (0,)), ((), ()))
    tn = (((0,), (0,)), ((), ()))
    dot = functools.partial(lax.dot_general, preferred_element_type=jnp.float32)
    stats = [
        piece[step * share : step * share + plan["stat_rows"], :].astype(jnp.float32)
        for piece, step in zip(pieces, steps)
    ]
    wide = 2 if count % 2 == 0 else 1
    total_rows = share * members
    if plan["sum_rows"] > total_rows:
        for at in range(count):
            sums[at, total_rows:, :] = jnp.zeros((plan["sum_rows"] - total_rows, BLOCK), jnp.float32)

    def own(side, head, which):
        top = 4 * BLOCK * head + (2 + which) * BLOCK
        return near[side][top : top + BLOCK, :]

    def rows(at, head, which):
        top = steps[at] * head + which * BLOCK
        return pieces[at][top : top + BLOCK, :]

    for head in range(share):
        for group in range(0, count, wide):
            ats = range(group, group + wide)
            queries = jnp.concatenate([rows(at, head, 0) for at in ats], axis=0)
            grads = jnp.concatenate([rows(at, head, 1) for at in ats], axis=0)
            line = jnp.concatenate([stats[at][4 * head : 4 * head + 4] for at in ats], axis=1)
            saved = (line[0:1] + line[1:2]) * LOG2E
            delta = line[2:3] + line[3:4]
            spot = slice(group * BLOCK, (group + wide) * BLOCK)
            for side in range(members):
                part = slice(side * BLOCK, (side + 1) * BLOCK)
                scores = dot(own(side, head, 0), queries, nt)
                weight_grads = dot(own(side, head, 1), grads, nt)
                shifts = [
                    jnp.full((1, BLOCK), shift[(places[at] * members + side) * share + head])
                    for at in ats
                ]
                offset = jnp.concatenate(shifts, axis=1) - saved
                weights = jnp.exp2(scores * (scale * LOG2E) + offset)
                score_grads = weights * (weight_grads - delta)
                weights_low[part, spot] = weights.astype(jnp.bfloat16)
                grads_low[part, spot] = score_grads.astype(jnp.bfloat16)
                column_sums = jnp.sum(score_grads, axis=0, keepdims=True)
                row = head * members + side
                for at in ats:
                    lanes = slice((at - group) * BLOCK, (at - group + 1) * BLOCK)
                    sums[at, row : row + 1, :] = column_sums[:, lanes]
        keys = jnp.concatenate([own(side, head, 0) for side in range(members)], axis=0)
        queries = jnp.concatenate([rows(at, head, 0) for at in range(count)], axis=0)
        grads = jnp.concatenate([rows(at, head, 1) for at in range(count)], axis=0)
        query_grad = dot(grads_low[...], keys, tn) * scale
        for at in range(count):
            outs[at][head * BLOCK : (head + 1) * BLOCK, :] = query_grad[
                at * BLOCK : (at + 1) * BLOCK
            ].astype(jnp.bfloat16)
        value_grad = dot(weights_low[...], grads, nn)
        key_grad = dot(grads_low[...], queries, nn)
        if before is not None:
            key_grad = key_grad + before[0][head]
            value_grad = value_grad + before[1][head]
        if last:
            key_grad = key_grad * scale
            top = 2 * BLOCK * head
            for side in range(members):
                part = slice(side * BLOCK, (side + 1) * BLOCK)
                owned[side][top : top + BLOCK, :] = key_grad[part].astype(jnp.bfloat16)
                owned[side][top + BLOCK : top + 2 * BLOCK, :] = value_grad[part].astype(jnp.bfloat16)
        else:
            after[0][head] = key_grad
            after[1][head] = value_grad
    lane = lax.broadcasted_iota(jnp.int32, (plan["sum_rows"], BLOCK), 1)
    for at in range(count):
        total = jnp.sum(sums[at], axis=1, keepdims=True)
        high, low = split_two(total)
        middle, low = split_two(low)
        spread = jnp.where(lane == 1, middle, jnp.where(lane == 2, low, 0.0))
        spread = jnp.where(lane == 0, high, spread)
        outs[at][share * BLOCK : share * BLOCK + plan["sum_rows"], :] = spread.astype(jnp.bfloat16)


def bias_kernel(plan, index, *refs):
    blocks, members, share, cells = plan["blocks"], plan["members"], plan["share"], plan["cells"]
    heads, per_cell = members * share, blocks // cells
    pieces, parts = refs[:blocks], refs[blocks : blocks + cells]
    slots, sums, table = refs[blocks + cells :]
    me, cell = lax.axis_index("gene"), lax.axis_index("cell")
    mine = me % members
    for slot in range(blocks):
        slots[index[me * blocks + slot]] = slot
    for hop in range(members):
        owner = mine ^ hop
        for other in range(hop, blocks, members):
            rows = pieces[other][share * BLOCK : share * BLOCK + plan["sum_rows"], :]
            rows = rows.astype(jnp.float32)
            for side in range(members):
                slot = slots[me ^ other ^ side]
                for head in range(share):
                    at = head * members + side
                    sums[pl.ds(slot * heads + owner * share + head, 1), :] = rows[at : at + 1]
    line = jnp.sum(jnp.transpose(sums[...]), axis=0, keepdims=True)
    for slot in range(blocks):
        table[slot : slot + 1, 0:heads] = line[:, slot * heads : (slot + 1) * heads]
    for hop in range(cells):
        for slot in range(per_cell):
            parts[hop][slot : slot + 1, :] = table[pl.ds((cell ^ hop) * per_cell + slot, 1), 0:heads]


def unpack_kernel(plan, *refs):
    blocks, members, share = plan["blocks"], plan["members"], plan["share"]
    head_size = plan["head_size"]
    pieces, owned = refs[:blocks], refs[blocks : blocks + members]
    query_grad, key_grad, value_grad, passed = refs[-4:]
    passed[...] = refs[blocks + members][...]
    mine = lax.axis_index("gene") % members
    for hop in range(members):
        start = pl.multiple_of((mine ^ hop) * (share * head_size), head_size)
        for head in range(share):
            columns = pl.ds(start + head * head_size, head_size)
            top = head * BLOCK
            total = pieces[hop][top : top + BLOCK, :].astype(jnp.float32)
            for other in range(members + hop, blocks, members):
                total = total + pieces[other][top : top + BLOCK, :].astype(jnp.float32)
            query_grad[0, :, columns] = total.astype(jnp.bfloat16)
            top = 2 * BLOCK * head
            key_grad[0, :, columns] = owned[hop][top : top + BLOCK, :]
            value_grad[0, :, columns] = owned[hop][top + BLOCK : top + 2 * BLOCK, :]


def call(kernel, outs, scratch=(), smem_in=0, smem_out=False, count=0, limit=VMEM_LIMIT, flops=None):
    places = [pl.BlockSpec(memory_space=pltpu.SMEM)] * smem_in
    places += [pl.BlockSpec(memory_space=pltpu.VMEM)] * count
    space = pltpu.SMEM if smem_out else pltpu.VMEM
    return pl.pallas_call(
        kernel,
        out_shape=outs,
        in_specs=places,
        out_specs=[pl.BlockSpec(memory_space=space)] * len(outs),
        scratch_shapes=list(scratch),
        compiler_params=pltpu.CompilerParams(vmem_limit_bytes=limit),
        cost_estimate=flops and pl.CostEstimate(flops=flops, bytes_accessed=0, transcendentals=0),
    )


def shards(
    query_rows,
    key_rows,
    value_rows,
    output_rows,
    output_grad,
    row_lse,
    block_bias,
    block_index,
    block_count,
):
    row_width = query_rows.shape[2]
    head_count = row_lse.shape[2]
    blocks = block_bias.shape[0]
    members = math.gcd(blocks, head_count)
    share = head_count // members
    head_size = row_width // head_count
    low, full = jnp.bfloat16, jnp.float32
    stat_rows = -(-4 * share // ROW_TILE) * ROW_TILE
    sum_rows = -(-share * members // ROW_TILE) * ROW_TILE
    far_rows = 2 * BLOCK * share + stat_rows
    plan = dict(
        blocks=blocks,
        members=members,
        share=share,
        head_size=head_size,
        stat_rows=stat_rows,
        sum_rows=sum_rows,
        far_rows=far_rows,
        scale=1.0 / math.sqrt(head_size),
    )

    cells = lax.axis_size("cell")
    plan["cells"] = cells
    near_rows = 4 * BLOCK * share + stat_rows
    near_in = jax.ShapeDtypeStruct((near_rows, BLOCK), low)
    far_in = jax.ShapeDtypeStruct((far_rows, BLOCK), low)
    sent = call(functools.partial(pack_kernel, plan), [near_in] * members + [far_in] * members, count=6)(
        query_rows, key_rows, value_rows, output_rows, output_grad, jnp.transpose(row_lse, (2, 0, 1))
    )

    def move(array, hop, axis="gene", size=blocks):
        return lax.ppermute(array, axis, [(i, i ^ hop) for i in range(size)])

    far = {hop: move(sent[members + hop % members], hop) for hop in range(members, blocks)}
    near = [sent[0]] + [move(sent[hop], hop) for hop in range(1, members)]
    (table,) = call(
        functools.partial(table_kernel, plan),
        [jax.ShapeDtypeStruct((blocks * members * share,), full)],
        smem_in=3,
        smem_out=True,
    )(block_bias.reshape(-1), block_index.reshape(-1), block_count)
    query_out = jax.ShapeDtypeStruct((share * BLOCK + sum_rows, BLOCK), low)
    partial_out = jax.ShapeDtypeStruct((share, members * BLOCK, BLOCK), full)
    owner_out = jax.ShapeDtypeStruct((2 * BLOCK * share, BLOCK), low)

    def stage(places, first, last, partials):
        count = len(places)
        pieces = [far[place] for place in places if place >= members]
        scratch = pltpu.VMEM((members * BLOCK, count * BLOCK), low)
        made = call(
            functools.partial(stage_kernel, plan, places, first, last),
            [query_out] * count + ([owner_out] * members if last else [partial_out] * 2),
            scratch=[scratch, scratch, pltpu.VMEM((count, sum_rows, BLOCK), full)],
            smem_in=1,
            count=members + len(pieces) + len(partials),
            limit=STAGE_LIMIT,
        )(table, *near, *pieces, *partials)
        return made[:count], made[count:]

    queries, partials, begin = [], [], 0
    for end in (members, members + (blocks - members) // 2, blocks):
        places = tuple(range(begin, end))
        made, partials = stage(places, begin == 0, end == blocks, partials)
        queries += [move(piece, place) if place else piece for piece, place in zip(made, places)]
        begin = end
    owned = [partials[0]] + [move(partials[hop], hop) for hop in range(1, members)]
    whole = jax.ShapeDtypeStruct((1, BLOCK, row_width), low)
    part_out = jax.ShapeDtypeStruct((blocks // cells, head_count), full)
    parts = call(
        functools.partial(bias_kernel, plan),
        [part_out] * cells,
        scratch=[
            pltpu.SMEM((blocks,), jnp.int32),
            pltpu.VMEM((head_count * blocks, BLOCK), full),
            pltpu.VMEM((blocks, BLOCK), full),
        ],
        smem_in=1,
        count=blocks,
        limit=STAGE_LIMIT,
        flops=40000000000,
    )(block_index.reshape(-1), *queries)
    query_grad, key_grad, value_grad, own_part = call(
        functools.partial(unpack_kernel, plan),
        [whole] * 3 + [part_out],
        count=blocks + members + 1,
        limit=STAGE_LIMIT,
    )(*queries, *owned, parts[0])
    parts = [own_part] + [move(parts[hop], hop, "cell", cells) for hop in range(1, cells)]
    bias_grad = jnp.transpose(functools.reduce(jnp.add, parts))[None]
    return (query_grad, key_grad, value_grad, bias_grad)


def solution(mesh):
    rows = P("cell", "gene", None)
    in_specs = (rows,) * 6 + (P(),) * 3
    out_specs = (rows, rows, rows, P("gene", None, "cell"))
    return jax.shard_map(shards, mesh=mesh, in_specs=in_specs, out_specs=out_specs, check_vma=False)
```
